128 devices in a mesh: group: 8 (over x, core), dom: 16 (over z, y).
Axes of the slice: x: 4, y: 4, z: 4, core: 2. Of those that a mesh axis runs over, the one named last changes fastest.
Arguments:
- node_input: bfloat16 [65536, 512], P(('group', 'dom')), may hold values from -24 to 24
- virtual_input: bfloat16 [64, 512], replicated, may hold values from -24 to 24
- w_query: bfloat16 [512, 512], replicated, may hold values from -0.25 to 0.25
- w_key: bfloat16 [512, 512], replicated, may hold values from -0.25 to 0.25
- w_value: bfloat16 [512, 512], replicated, may hold values from -0.25 to 0.25
- w_out: bfloat16 [512, 512], replicated, may hold values from -0.25 to 0.25
- w_up: bfloat16 [512, 2048], replicated, may hold values from -0.25 to 0.25
- w_down: bfloat16 [2048, 512], replicated, may hold values from -0.125 to 0.125
- gain_attn: float32 [512], replicated, may hold values from 0.25 to 1.75
- gain_ffn: float32 [512], replicated, may hold values from 0.25 to 1.75
- local_nbr: int32 [65536, 8], P(('group', 'dom')), may hold values from 0 to 767, as said below
- local_len: int32 [65536], P(('group', 'dom')), may hold values from 1 to 8
- send_rows: int32 [128, 128, 16], P(('group', 'dom')), may hold values from 0 to 511
- exp_slot: int32 [65536, 4], P(('group', 'dom')), may hold values from 0 to 2047, as said below
- membership: int32 [65536], P(('group', 'dom')), may hold values from 0 to 63
Outputs:
- node_output: bfloat16 [65536, 512], P(('group', 'dom'))
- virtual_output: bfloat16 [64, 512], replicated
The draws below stay inside these ranges and needn't reach their ends.
Inputs may be any that keep to these rules, and one draw needn't show every extreme that they name: `local_nbr`: positions 0 to 127 are the last 128 nodes of the previous shard of the same group (dom index one lower, cyclically), 128 to 639 the node's own shard, and the rest the first 128 nodes of the next shard. `exp_slot`: slot s of a receiving device is row s mod 16 of the block from device s // 16; the nodes of one device name every one of its 2048 slots exactly once.
All inputs are finite; a program needn't handle non-finite values.
Results may differ from the reference program's by a relative error of at most 0.024.
The reference program's roundings to bfloat16 on the way (of `attention`, `settled`, `hidden` and `v_attention`) count: a program that leaves them out, or rounds other values in their place, can miss the bound.
Values may be sent and summed in bfloat16 or wider, within the bound.
A program may use at most 128 MiB of HBM per device.

```python
import math
import jax
import jax.numpy as jnp
from jax import lax

D = 512
HEADS = 8
FF = 2048
VN = 64
LDEG = 8
EXP_DEG = 4
HALO = 128
NODE_DEV = 512
PEERS = 128
NODES = 65536
CAP = 16
N_DOM = 16


def draw_node_input(key, part):
    key = jax.random.fold_in(key, 11)
    values = jax.random.normal(key, (NODES, D), jnp.float32)
    return jnp.clip(values, -24.0, 24.0).astype(jnp.bfloat16)


def draw_virtual_input(key, part):
    key = jax.random.fold_in(key, 12)
    values = jax.random.normal(key, (VN, D), jnp.float32)
    return jnp.clip(values, -24.0, 24.0).astype(jnp.bfloat16)


def draw_local_nbr(key, part):
    key = jax.random.fold_in(key, 13)
    key_inner, key_rim, key_pick = jax.random.split(key, 3)
    inner = jax.random.randint(key_inner, (NODES, LDEG), HALO, HALO + NODE_DEV, dtype=jnp.int32)
    rim = jax.random.randint(key_rim, (NODES, LDEG), 0, 2 * HALO, dtype=jnp.int32)
    rim = jnp.where(rim < HALO, rim, rim + NODE_DEV)
    pick = jax.random.randint(key_pick, (NODES, LDEG), 0, 4, dtype=jnp.int32)
    return jnp.where(pick == 0, rim, inner).astype(jnp.int32)


def draw_exp_slot(key, part):
    key = jax.random.fold_in(key, 14)
    device_keys = jax.random.split(key, NODES // NODE_DEV)
    perms = jax.vmap(lambda one_key: jax.random.permutation(one_key, EXP_DEG * NODE_DEV))(device_keys)
    return perms.reshape(NODES, EXP_DEG).astype(jnp.int32)


def draw_membership(key, part):
    key = jax.random.fold_in(key, 15)
    key_near, key_far, key_pick = jax.random.split(key, 3)
    device = jnp.arange(NODES, dtype=jnp.int32) // NODE_DEV
    base = device * VN // (NODES // NODE_DEV)
    near = (base + jax.random.randint(key_near, (NODES,), 0, 4, dtype=jnp.int32)) % VN
    far = jax.random.randint(key_far, (NODES,), 0, VN, dtype=jnp.int32)
    pick = jax.random.randint(key_pick, (NODES,), 0, 8, dtype=jnp.int32)
    return jnp.where(pick == 0, far, near).astype(jnp.int32)


def touch_ends(entries, key, least, high):
    dims = entries.shape
    place = [jax.random.randint(jax.random.fold_in(key, axis), (), 0, dims[axis]) for axis in range(len(dims))]
    entries = entries.at[tuple(place)].set(least)
    longest = dims.index(max(dims))
    place[longest] = (place[longest] + 1) % dims[longest]
    return entries.at[tuple(place)].set(high)


def centred(key, dims, scale, most, kind=jnp.bfloat16):
    values = scale * jax.random.normal(key, dims, jnp.float32)
    return jnp.clip(values, min=-most, max=most).astype(kind)


def setup_inputs(seed: int = 0) -> dict:
    key_of = jax.random.split(jax.random.key(seed), 16)
    return {
        "node_input": draw_node_input(jax.random.fold_in(key_of[15], 71), 0),
        "virtual_input": draw_virtual_input(jax.random.fold_in(key_of[15], 71), 0),
        "w_query": centred(key_of[2], (D, D), D ** -0.5, 0.25),
        "w_key": centred(key_of[3], (D, D), D ** -0.5, 0.25),
        "w_value": centred(key_of[4], (D, D), D ** -0.5, 0.25),
        "w_out": centred(key_of[5], (D, D), D ** -0.5, 0.25),
        "w_up": centred(key_of[6], (D, FF), D ** -0.5, 0.25),
        "w_down": centred(key_of[7], (FF, D), FF ** -0.5, 0.125),
        "gain_attn": jnp.clip(1.0 + 0.15 * jax.random.normal(key_of[8], (D,), jnp.float32), 0.25, 1.75),
        "gain_ffn": jnp.clip(1.0 + 0.15 * jax.random.normal(key_of[9], (D,), jnp.float32), 0.25, 1.75),
        "local_nbr": draw_local_nbr(jax.random.fold_in(key_of[15], 71), 0),
        "local_len": touch_ends(jax.random.randint(key_of[11], (NODES,), 1, LDEG + 1), jax.random.fold_in(key_of[11], 1), 1, LDEG).astype(jnp.int32),
        "send_rows": touch_ends(jax.random.randint(key_of[12], (PEERS, PEERS, CAP), 0, NODE_DEV), jax.random.fold_in(key_of[12], 1), 0, NODE_DEV - 1).astype(jnp.int32),
        "exp_slot": draw_exp_slot(jax.random.fold_in(key_of[15], 71), 0),
        "membership": draw_membership(jax.random.fold_in(key_of[15], 71), 0),
    }


def layer_norm(summed, scaling):
    center = summed - lax.optimization_barrier(jnp.mean(summed, axis=-1, keepdims=True))
    spread = lax.optimization_barrier(jnp.mean(center * center, axis=-1, keepdims=True))
    return center * lax.rsqrt(spread + 1e-05) * scaling

def head_scores(queries, targets, head_count):
    product = queries.astype(jnp.float32) * targets.astype(jnp.float32)
    product = product.reshape(product.shape[0], head_count, -1)
    return lax.optimization_barrier(jnp.sum(product, axis=-1)) / math.sqrt(product.shape[2])

def project(inputs, weight_one):
    return jnp.dot(inputs, weight_one, preferred_element_type=jnp.float32).astype(jnp.bfloat16)

def reference(node_input, virtual_input, w_query, w_key, w_value, w_out, w_up, w_down, gain_attn, gain_ffn, local_nbr, local_len, send_rows, exp_slot, membership):
    node_count, feat_width = node_input.shape
    head_size = feat_width // HEADS
    slot_cap = send_rows.shape[2]
    queries = project(node_input, w_query)
    keys_all = project(node_input, w_key)
    values_all = project(node_input, w_value)
    v_query = project(virtual_input, w_query)
    v_keys = project(virtual_input, w_key)
    v_values = project(virtual_input, w_value)
    node_index = jnp.arange(node_count, dtype=jnp.int32)
    device = node_index // NODE_DEV
    cycle_len = NODE_DEV * N_DOM
    group_base = device // N_DOM * cycle_len
    offset = device % N_DOM * NODE_DEV - HALO
    local_ids = group_base[:, None] + jnp.mod(offset[:, None] + local_nbr, cycle_len)
    source = exp_slot // slot_cap
    column = exp_slot % slot_cap
    expander_ids = source * NODE_DEV + send_rows[source, device[:, None], column]
    neighbours = jnp.concatenate([local_ids, expander_ids], axis=1).astype(jnp.int32)
    onehot = (membership[:, None] == jnp.arange(VN, dtype=jnp.int32)[None, :]).astype(jnp.bfloat16)
    own_key = project(onehot, v_keys)
    own_value = project(onehot, v_values)
    slot_count = neighbours.shape[1]
    score_list = [head_scores(queries, keys_all[neighbours[:, slot_idx]], HEADS) for slot_idx in range(slot_count)]
    score_list.append(head_scores(queries, own_key, HEADS))
    scores = jnp.stack(score_list, axis=1)
    allowed = jnp.concatenate([jnp.arange(LDEG, dtype=jnp.int32)[None, :] < local_len[:, None], jnp.ones((node_count, EXP_DEG + 1), dtype=bool)], axis=1)
    masked = jnp.where(allowed[:, :, None], scores, -1e+30)
    peak_score = lax.optimization_barrier(jnp.max(masked, axis=1, keepdims=True))
    raised = jnp.exp(masked - peak_score)
    weights = raised / lax.optimization_barrier(jnp.sum(raised, axis=1, keepdims=True))
    attention = jnp.zeros((node_count, HEADS, head_size), jnp.float32)
    for slot_idx in range(slot_count + 1):
        if slot_idx < slot_count:
            picked = values_all[neighbours[:, slot_idx]]
        else:
            picked = own_value
        attention = attention + weights[:, slot_idx, :, None] * picked.astype(jnp.float32).reshape(node_count, HEADS, head_size)
    attention = attention.reshape(node_count, feat_width).astype(jnp.bfloat16)
    mixed = node_input.astype(jnp.float32) + jnp.dot(attention, w_out, preferred_element_type=jnp.float32)
    settled = layer_norm(mixed, gain_attn).astype(jnp.bfloat16)
    hidden = jnp.maximum(jnp.dot(settled, w_up, preferred_element_type=jnp.float32), 0.0).astype(jnp.bfloat16)
    node_output = layer_norm(settled.astype(jnp.float32) + jnp.dot(hidden, w_down, preferred_element_type=jnp.float32), gain_ffn).astype(jnp.bfloat16)
    vq_heads = v_query.astype(jnp.float32).reshape(VN, HEADS, head_size)
    vk_heads = v_keys.astype(jnp.float32).reshape(VN, HEADS, head_size)
    vv_heads = v_values.astype(jnp.float32).reshape(VN, HEADS, head_size)
    key_heads = keys_all.astype(jnp.float32).reshape(node_count, HEADS, head_size)
    value_heads = values_all.astype(jnp.float32).reshape(node_count, HEADS, head_size)
    member_scores = jnp.einsum('vhc,nhc->vhn', vq_heads, key_heads, precision=lax.Precision.HIGHEST) / math.sqrt(head_size)
    member = membership[None, None, :] == jnp.arange(VN, dtype=jnp.int32)[:, None, None]
    member_masked = jnp.where(member, member_scores, -1e+30)
    self_score = lax.optimization_barrier(jnp.sum(vq_heads * vk_heads, axis=-1)) / math.sqrt(head_size)
    v_peak = jnp.maximum(lax.optimization_barrier(jnp.max(member_masked, axis=2)), self_score)
    v_raised = jnp.exp(member_masked - v_peak[:, :, None])
    self_raised = jnp.exp(self_score - v_peak)
    v_total = lax.optimization_barrier(jnp.sum(v_raised, axis=2)) + self_raised
    v_acc = jnp.einsum('vhn,nhc->vhc', v_raised, value_heads, precision=lax.Precision.HIGHEST) + self_raised[:, :, None] * vv_heads
    v_attention = (v_acc / v_total[:, :, None]).reshape(VN, feat_width).astype(jnp.bfloat16)
    v_mixed = virtual_input.astype(jnp.float32) + jnp.dot(v_attention, w_out, preferred_element_type=jnp.float32)
    virtual_output = layer_norm(v_mixed, gain_attn).astype(jnp.bfloat16)
    return (node_output, virtual_output)
```

```python
import functools

import jax
import jax.numpy as jnp
from jax import lax
from jax.experimental import pallas as pl
from jax.experimental.pallas import tpu as pltpu
from jax.sharding import PartitionSpec as P

MESH = pl.DeviceIdType.MESH
BF = jnp.bfloat16
F32 = jnp.float32
NEG = -1e30

D = 512
H = 8
HD = D // H
N = 512
VN = 64
HALO = 128
CAP = 16
BLK = 256
OWN_BLOCKS = N // BLK
FIRST_EXP = OWN_BLOCKS + 1
GROUPS = 8
BLOCKS = FIRST_EXP + GROUPS
ROWS = BLOCKS * BLK
EXP0 = FIRST_EXP * BLK
PART = D + 256


def dot(a, b, dims=((1,), (0,)), precision=None):
    return lax.dot_general(a, b, (dims, ((), ())), precision=precision, preferred_element_type=F32)


NT = ((1,), (1,))


def iota(shape, dim):
    return lax.broadcasted_iota(jnp.int32, shape, dim)


def norm(u, gain):
    center = u - jnp.mean(u, axis=-1, keepdims=True)
    spread = jnp.mean(center * center, axis=-1, keepdims=True)
    return center * lax.rsqrt(spread + 1e-05) * gain


def expander(rows):
    return (iota((rows, D), 1) // HD == iota((rows, D), 0)).astype(F32)


def wrap(value, size):
    return jnp.where(value >= size, value - size, value)


def kernel(
    x_hbm, vx_hbm, wq_hbm, wk_hbm, wv_hbm, wo_hbm, wu_hbm, wd_hbm, ga_hbm, gf_hbm,
    nbr_hbm, len_hbm, rows_hbm, slot_hbm, mem_hbm,
    out_hbm, vout_hbm,
    xall, vx, wq, wk, wv, wo, wu, wd, ga, gf, nbr, length, rows, slot, mem,
    send, wvt, qm, bias, kblk, vt, m_ref, l_ref, acc, att, outs,
    vq32, vk32, vv32, vkey, vbias, part, r1, c1, r2, r3a, r3, vrow, vout,
    in_sem, out_sem, ssem, rsem, halo_s, halo_r, s1s, s1r, s2s, s2r, s3s, s3r, s4s, s4r,
):
    g = lax.axis_index("group")
    d = lax.axis_index("dom")
    x, c = g // 2, g % 2
    z, y = d // 4, d % 4

    order = [
        (x_hbm, xall.at[pl.ds(0, N)]), (rows_hbm, rows), (wq_hbm, wq), (wk_hbm, wk), (wv_hbm, wv),
        (vx_hbm, vx), (mem_hbm, mem), (len_hbm, length), (nbr_hbm, nbr), (slot_hbm, slot),
        (ga_hbm, ga), (gf_hbm, gf), (wo_hbm, wo), (wu_hbm, wu), (wd_hbm, wd),
    ]
    loads = [pltpu.make_async_copy(a, b, in_sem.at[i]) for i, (a, b) in enumerate(order)]
    for load in loads:
        load.start()

    barrier = pltpu.get_barrier_semaphore()
    others = [wrap(g + i, H) for i in range(8)]

    def greet(dom, first):
        for i in range(first, 8):
            pl.semaphore_signal(barrier, inc=1, device_id=(others[i], dom), device_id_type=MESH)

    greet(d, 1)

    def greet_dom(i, carry):
        greet(wrap(d + i, 16), 0)
        return carry

    lax.fori_loop(1, 16, greet_dom, 0)

    loads[0].wait()
    loads[1].wait()
    picks = rows[...]
    lanes16 = iota((CAP, N), 1)
    for chunk in range(8):
        hot = jnp.concatenate(
            [
                (picks[:, chunk * 16 + i : chunk * 16 + i + 1] == lanes16).astype(F32).astype(BF)
                for i in range(16)
            ],
            axis=0,
        )
        send[pl.ds(chunk * 256, 256), :] = dot(hot, xall[pl.ds(0, N), :]).astype(BF)

    pl.semaphore_wait(barrier, 127)

    up, down = wrap(d + 1, 16), wrap(d + 15, 16)
    to_up = pltpu.make_async_remote_copy(
        xall.at[pl.ds(N - HALO, HALO)], xall.at[pl.ds(N + HALO, HALO)],
        halo_s.at[0], halo_r.at[0], device_id=(g, up), device_id_type=MESH,
    )
    to_down = pltpu.make_async_remote_copy(
        xall.at[pl.ds(0, HALO)], xall.at[pl.ds(N, HALO)],
        halo_s.at[1], halo_r.at[1], device_id=(g, down), device_id_type=MESH,
    )
    to_up.start()
    to_down.start()

    ty = [wrap(y + i, 4) for i in range(4)]
    tc = [c, 1 - c]

    def post(group, kz, first):
        kc, jx = group % 2, group // 2
        tz = wrap(z + kz, 4)
        xb = wrap(x + kz, 4)
        for ky in range(first, 4):
            tg = wrap(xb + (jx + ky) % 4, 4) * 2 + tc[kc]
            td = tz * 4 + ty[ky]
            pltpu.make_async_remote_copy(
                send.at[pl.ds(pl.multiple_of((tg * 16 + td) * CAP, CAP), CAP)],
                xall.at[pl.ds(pl.multiple_of(EXP0 + group * BLK + (kz * 4 + ky) * CAP, CAP), CAP)],
                ssem, rsem.at[group], device_id=(tg, td), device_id_type=MESH,
            ).start()

    for group in range(GROUPS):
        if group == 0:
            post(0, 0, 1)

        def post_z(kz, carry):
            post(group, kz, 0)
            return carry

        lax.fori_loop(1 if group == 0 else 0, 4, post_z, 0)
    me = g * 16 + d
    xall[pl.ds(EXP0, CAP), :] = send[pl.ds(pl.multiple_of(me * CAP, CAP), CAP), :]

    for i in range(2, 12):
        loads[i].wait()
    half = iota((BLK, 128), 1) // HD
    for r in range(0, N, BLK):
        q = (dot(xall[pl.ds(r, BLK), :], wq[...]).astype(BF) * 0.125).astype(F32)
        for h in range(H):
            pair = q[:, h // 2 * 128 : h // 2 * 128 + 128]
            qm[h, pl.ds(r, BLK), :] = jnp.where(half == h % 2, pair, 0.0).astype(BF)
    wvt[...] = wv[...].T
    vq32[...] = dot(vx[...], wq[...]).astype(BF).astype(F32) * 0.125
    vkey[...] = dot(vx[...], wk[...]).astype(BF)
    vk32[...] = vkey[...].astype(F32)
    vval = dot(vx[...], wv[...]).astype(BF)
    vv32[...] = vval.astype(F32)

    member_row = mem[...]
    member = iota((VN, N), 0) == member_row
    k_own = dot(xall[pl.ds(0, N), :], wk[...]).astype(BF)
    v_own = dot(xall[pl.ds(0, N), :], wv[...]).astype(BF)
    head_of = iota((VN, D), 1) // HD
    lane = iota((VN, 128), 1)
    part_acc = jnp.zeros((VN, D), F32)
    part_max = jnp.zeros((VN, 128), F32)
    part_sum = jnp.zeros((VN, 128), F32)
    for h in range(H):
        pair = slice(h // 2 * 128, h // 2 * 128 + 128)
        vqh = jnp.where(head_of == h, vq32[...], 0.0).astype(BF)[:, pair]
        s = jnp.where(member, dot(vqh, k_own[:, pair], NT), NEG)
        top = jnp.max(s, axis=1, keepdims=True)
        p = jnp.where(member, jnp.exp(s - top), 0.0)
        part_max = jnp.where(lane == h, top, part_max)
        part_sum = jnp.where(lane == h, jnp.sum(p, axis=1, keepdims=True), part_sum)
        high = p.astype(BF)
        low = (p - high.astype(F32)).astype(BF)
        o = dot(high, v_own) + dot(low, v_own)
        part_acc = jnp.where(head_of == h, o, part_acc)
    part[:, pl.ds(0, D)] = part_acc
    part[:, pl.ds(D, 128)] = part_max
    part[:, pl.ds(D + 128, 128)] = part_sum
    for i in range(1, 8):
        pltpu.make_async_remote_copy(
            part.at[pl.ds(pl.multiple_of(others[i] * 8, 8), 8)], r1.at[g],
            s1s, s1r, device_id=(others[i], d), device_id_type=MESH,
        ).start()
    r1[g] = part[pl.ds(pl.multiple_of(g * 8, 8), 8), :]

    win = nbr[...] - HALO
    win = jnp.where(win < 0, win + EXP0, win)
    win = jnp.where(iota((8, N), 0) < length[...], win, -1)
    for r in range(0, EXP0, 64):
        row = iota((64, N), 0) + r
        count = jnp.zeros((64, N), F32)
        for e in range(8):
            count = count + jnp.where(win[e : e + 1, :] == row, 1.0, 0.0)
        bias[pl.ds(r, 64), :] = jnp.where(count > 0.0, jnp.log(jnp.maximum(count, 1.0)), NEG)
    source = slot[...] // CAP
    sg, sd = source // 16, source % 16
    kz = (z - sd // 4 + 4) % 4
    ky = (y - sd % 4 + 4) % 4
    kc = (c - sg % 2 + 2) % 2
    kx = (x - sg // 2 + 4) % 4
    jx = (kx - kz - ky + 8) % 4
    spot = (jx * 2 + kc) * BLK + (kz * 4 + ky) * CAP + slot[...] % CAP

    def expander_bias(i, carry):
        r = pl.multiple_of(i * 64, 64)
        row = iota((64, N), 0) + r
        hit = spot[0:1, :] == row
        for e in range(1, 4):
            hit = hit | (spot[e : e + 1, :] == row)
        bias[pl.ds(EXP0 + r, 64), :] = jnp.where(hit, 0.0, NEG)
        return carry

    lax.fori_loop(0, GROUPS * BLK // 64, expander_bias, 0)

    vvt = vval.T
    vbias[...] = jnp.where(member, 0.0, NEG)
    for h in range(H):
        pair = slice(h // 2 * 128, h // 2 * 128 + 128)
        s = dot(vkey[:, pair], qm[h], NT) + vbias[...]
        top = jnp.max(s, axis=0, keepdims=True)
        p = jnp.exp(s - top)
        m_ref[h : h + 1, :] = top
        l_ref[h : h + 1, :] = jnp.sum(p, axis=0, keepdims=True)
        acc[h * HD : (h + 1) * HD, :] = dot(vvt[h * HD : (h + 1) * HD, :], p.astype(BF))

    def wait_bytes(like, sem):
        pltpu.make_async_copy(like, like, sem).wait()

    expand = expander(128)

    def combine(parts):
        tops = [q[:, D : D + 128] for q in parts]
        top = functools.reduce(jnp.maximum, tops)
        scale = [jnp.exp(t - top) for t in tops]
        total = functools.reduce(jnp.add, [q[:, D + 128 :] * f for q, f in zip(parts, scale)])
        wide = dot(jnp.concatenate(scale, axis=0), expand, precision=lax.Precision.HIGHEST)
        n = parts[0].shape[0]
        mixed = functools.reduce(
            jnp.add, [q[:, :D] * wide[i * n : (i + 1) * n, :] for i, q in enumerate(parts)]
        )
        return mixed, top, total

    def block(b, carry):
        @pl.when(b == OWN_BLOCKS)
        def _():
            to_up.wait_recv()
            to_down.wait_recv()

        @pl.when(b == FIRST_EXP)
        def _():
            wait_bytes(xall.at[pl.ds(EXP0, 15 * CAP)], rsem.at[0])

        @pl.when(b > FIRST_EXP)
        def _():
            wait_bytes(xall.at[pl.ds(EXP0, 16 * CAP)], rsem.at[b - FIRST_EXP])

        @pl.when(b == FIRST_EXP)
        def _():
            wait_bytes(r1.at[pl.ds(0, 7)], s1r)
            mixed, top, total = combine([r1[i] for i in range(8)])
            for i in range(8):
                c1[i, :, pl.ds(0, D)] = mixed[i : i + 1, :]
                c1[i, :, pl.ds(D, 128)] = top[i : i + 1, :]
                c1[i, :, pl.ds(D + 128, 128)] = total[i : i + 1, :]

            for i in range(8):
                @pl.when(d != i)
                def _():
                    pltpu.make_async_remote_copy(
                        c1.at[i], r2.at[d], s2s, s2r, device_id=(g, i), device_id_type=MESH
                    ).start()

            @pl.when(d < 8)
            def _():
                r2[d] = c1[d]

        @pl.when((b == FIRST_EXP + 2) & (d < 8))
        def _():
            wait_bytes(r2.at[pl.ds(0, 15)], s2r)
            mixed, top, total = combine([r2[i] for i in range(16)])
            v = g * 8 + d
            vq, vk, vv = vq32[pl.ds(v, 1), :], vk32[pl.ds(v, 1), :], vv32[pl.ds(v, 1), :]
            eight = lambda row: jnp.broadcast_to(row, (8, row.shape[1]))
            own = dot(eight(vq * vk), expand, NT, precision=lax.Precision.HIGHEST)[0:1, :]
            peak = jnp.maximum(top, own)
            old, new = jnp.exp(top - peak), jnp.exp(own - peak)
            denom = total * old + new
            factors = jnp.concatenate([old, new, denom], axis=0)
            factors = jnp.concatenate([factors, jnp.zeros((5, 128), F32)], axis=0)
            wide = dot(factors, expand, precision=lax.Precision.HIGHEST)
            va = (mixed * wide[0:1, :] + wide[1:2, :] * vv) / wide[2:3, :]
            proj = dot(eight(va).astype(BF), wo[...])
            u = eight(vx_row(v)) + proj
            vrow[0] = norm(u, ga[...]).astype(BF).astype(F32)[0:1, :]
            for i in range(1, 16):
                pltpu.make_async_remote_copy(
                    vrow.at[0], r3a.at[d], s3s, s3r,
                    device_id=(g, wrap(d + i, 16)), device_id_type=MESH,
                ).start()
            r3a[d] = vrow[0]

        @pl.when(b == FIRST_EXP + 5)
        def _():
            @pl.when(d < 8)
            def _():
                wait_bytes(r3a.at[pl.ds(0, 7)], s3r)

            @pl.when(d >= 8)
            def _():
                wait_bytes(r3a.at[pl.ds(0, 8)], s3r)

            r3[g] = r3a[:, 0, :]
            for i in range(1, 8):
                pltpu.make_async_remote_copy(
                    r3.at[g], r3.at[g], s4s, s4r, device_id=(others[i], d), device_id_type=MESH
                ).start()

        r = pl.multiple_of(b * BLK, BLK)
        xb = xall[pl.ds(r, BLK), :]
        kblk[...] = dot(xb, wk[...]).astype(BF)
        vt[...] = dot(wvt[...], xb, NT).astype(BF)
        for h in range(H):
            pair = slice(h // 2 * 128, h // 2 * 128 + 128)
            s = dot(kblk[:, pair], qm[h], NT) + bias[pl.ds(r, BLK), :]
            old = m_ref[h : h + 1, :]
            top = jnp.maximum(old, jnp.max(s, axis=0, keepdims=True))
            keep = jnp.exp(old - top)
            p = jnp.exp(s - top)
            m_ref[h : h + 1, :] = top
            l_ref[h : h + 1, :] = l_ref[h : h + 1, :] * keep + jnp.sum(p, axis=0, keepdims=True)
            span = slice(h * HD, (h + 1) * HD)
            acc[span, :] = acc[span, :] * keep + dot(vt[span, :], p.astype(BF))
        return carry

    def vx_row(v):
        return vx32_row(vx, v)

    loads[12].wait()
    lax.fori_loop(0, BLOCKS, block, 0)

    for h in range(H):
        span = slice(h * HD, (h + 1) * HD)
        att[span, :] = (acc[span, :] * (1.0 / l_ref[h : h + 1, :])).astype(BF)
    loads[13].wait()
    loads[14].wait()
    attn = att[...].T
    att[...] = attn
    for r in range(0, N, BLK):
        at = pl.ds(r, BLK)
        mixed = xall[at, :].astype(F32) + dot(att[at, :], wo[...])
        settled = norm(mixed, ga[...]).astype(BF)
        total = settled.astype(F32)
        for f in range(0, 4 * D, D):
            hidden = jnp.maximum(dot(settled, wu[:, f : f + D]), 0.0).astype(BF)
            total = total + dot(hidden, wd[f : f + D, :])
        outs[at, :] = norm(total, gf[...]).astype(BF)
        pltpu.make_async_copy(outs.at[at], out_hbm.at[at], out_sem.at[r // BLK]).start()

    wait_bytes(r3.at[pl.ds(0, 7)], s4r)
    vout[...] = r3[...].reshape(VN, D).astype(BF)
    last = pltpu.make_async_copy(vout, vout_hbm, out_sem.at[2])
    last.start()

    to_up.wait_send()
    to_down.wait_send()
    wait_bytes(send.at[pl.ds(0, 127 * CAP)], ssem)
    wait_bytes(part.at[pl.ds(0, 56)], s1s)

    @pl.when(d < 8)
    def _():
        wait_bytes(c1.at[pl.ds(0, 7)], s2s)
        wait_bytes(r2.at[pl.ds(0, 15), :, pl.ds(0, D)], s3s)

    @pl.when(d >= 8)
    def _():
        wait_bytes(c1, s2s)

    wait_bytes(r3.at[pl.ds(0, 7)], s4s)
    for r in range(0, N, BLK):
        at = pl.ds(r, BLK)
        pltpu.make_async_copy(outs.at[at], out_hbm.at[at], out_sem.at[r // BLK]).wait()
    last.wait()


def vx32_row(vx, v):
    hot = (iota((8, VN), 1) == v).astype(F32).astype(BF)
    return dot(hot, vx[...])[0:1, :]


def shards(
    node_input, virtual_input, w_query, w_key, w_value, w_out, w_up, w_down, gain_attn, gain_ffn,
    local_nbr, local_len, send_rows, exp_slot, membership,
):
    args = (
        node_input, virtual_input, w_query, w_key, w_value, w_out, w_up, w_down,
        gain_attn.reshape(1, D), gain_ffn.reshape(1, D), local_nbr.T, local_len.reshape(1, N),
        send_rows[0].T, exp_slot.T, membership.reshape(1, N),
    )
    vmem = pltpu.VMEM
    dma = pltpu.SemaphoreType.DMA
    scratch = [
        vmem((ROWS, D), BF), vmem((VN, D), BF), vmem((D, D), BF), vmem((D, D), BF),
        vmem((D, D), BF), vmem((D, D), BF), vmem((D, 4 * D), BF), vmem((4 * D, D), BF),
        vmem((1, D), F32), vmem((1, D), F32), vmem((8, N), jnp.int32), vmem((1, N), jnp.int32),
        vmem((CAP, 128), jnp.int32), vmem((4, N), jnp.int32), vmem((1, N), jnp.int32),
        vmem((128 * CAP, D), BF), vmem((D, D), BF), vmem((H, N, 128), BF), vmem((ROWS, N), F32),
        vmem((BLK, D), BF), vmem((D, BLK), BF), vmem((H, N), F32), vmem((H, N), F32),
        vmem((D, N), F32), vmem((D, N), BF), vmem((N, D), BF),
        vmem((VN, D), F32), vmem((VN, D), F32), vmem((VN, D), F32), vmem((VN, D), BF),
        vmem((VN, N), F32), vmem((VN, PART), F32), vmem((8, 8, PART), F32),
        vmem((8, 1, PART), F32), vmem((16, 1, PART), F32), vmem((8, 1, D), F32),
        vmem((8, 8, D), F32), vmem((1, 1, D), F32), vmem((VN, D), BF),
        dma((15,)), dma((3,)), dma, dma((GROUPS,)), dma((2,)), dma((2,)),
        dma, dma, dma, dma, dma, dma, dma, dma,
    ]
    hbm = pl.BlockSpec(memory_space=pl.ANY)
    return pl.pallas_call(
        kernel,
        out_shape=(
            jax.ShapeDtypeStruct((N, D), BF),
            jax.ShapeDtypeStruct((VN, D), BF),
        ),
        in_specs=[hbm] * len(args),
        out_specs=(hbm, hbm),
        scratch_shapes=scratch,
        compiler_params=pltpu.CompilerParams(
            collective_id=0, has_side_effects=True, vmem_limit_bytes=56 * 1024 * 1024
        ),
    )(*args)


def solution(mesh):
    rows = P(("group", "dom"), None)
    line = P(("group", "dom"))
    placed = (
        rows, P(), P(), P(), P(), P(), P(), P(), P(), P(),
        rows, line, P(("group", "dom"), None, None), rows, line,
    )
    return jax.shard_map(
        shards, mesh=mesh, in_specs=placed, out_specs=(rows, P()), check_vma=False
    )
```

```python
import functools

import jax
import jax.numpy as jnp
from jax import lax
from jax.experimental import pallas as pl
from jax.experimental.pallas import tpu as pltpu
from jax.sharding import PartitionSpec as P

MESH = pl.DeviceIdType.MESH
BF = jnp.bfloat16
F32 = jnp.float32
NEG = -1e30

D = 512
H = 8
HD = D // H
N = 512
VN = 64
HALO = 128
CAP = 16
BLK = 256
OWN_BLOCKS = N // BLK
FIRST_EXP = OWN_BLOCKS + 1
GROUPS = 8
BLOCKS = FIRST_EXP + GROUPS
ROWS = BLOCKS * BLK
EXP0 = FIRST_EXP * BLK
PART = D + 256
VR = HD + 16
AR = HD + 8


def dot(a, b, dims=((1,), (0,)), precision=None):
    return lax.dot_general(a, b, (dims, ((), ())), precision=precision, preferred_element_type=F32)


NT = ((1,), (1,))


def iota(shape, dim):
    return lax.broadcasted_iota(jnp.int32, shape, dim)


def norm(u, gain):
    center = u - jnp.mean(u, axis=-1, keepdims=True)
    spread = jnp.mean(center * center, axis=-1, keepdims=True)
    return center * lax.rsqrt(spread + 1e-05) * gain


def expander(rows):
    return (iota((rows, D), 1) // HD == iota((rows, D), 0)).astype(F32)


def wrap(value, size):
    return jnp.where(value >= size, value - size, value)


def kernel(
    x_hbm, vx_hbm, wq_hbm, wk_hbm, wv_hbm, wo_hbm, wu_hbm, wd_hbm, ga_hbm, gf_hbm,
    nbr_hbm, len_hbm, rows_hbm, slot_hbm, mem_hbm,
    out_hbm, vout_hbm,
    xall, vx, wq, wk, wv, wo, wu, wd, ga, gf, nbr, length, rows, slot, mem,
    send, wvt, qm, bias, kblk, vt, m_ref, acc, att, outs,
    vq32, vk32, vv32, vkey, vbias, part, r1, c1, r2, r3a, r3, vrow, vout,
    in_sem, out_sem, ssem, rsem, halo_s, halo_r, s1s, s1r, s2s, s2r, s3s, s3r, s4s, s4r,
):
    g = lax.axis_index("group")
    d = lax.axis_index("dom")
    x, c = g // 2, g % 2
    z, y = d // 4, d % 4

    order = [
        (x_hbm, xall.at[pl.ds(0, N)]), (rows_hbm, rows), (wq_hbm, wq), (wk_hbm, wk), (wv_hbm, wv),
        (vx_hbm, vx), (mem_hbm, mem), (len_hbm, length), (nbr_hbm, nbr), (slot_hbm, slot),
        (ga_hbm, ga), (gf_hbm, gf), (wo_hbm, wo), (wu_hbm, wu), (wd_hbm, wd),
    ]
    loads = [pltpu.make_async_copy(a, b, in_sem.at[i]) for i, (a, b) in enumerate(order)]
    for load in loads:
        load.start()

    barrier = pltpu.get_barrier_semaphore()
    others = [wrap(g + i, H) for i in range(8)]

    def greet(dom, first):
        for i in range(first, 8):
            pl.semaphore_signal(barrier, inc=1, device_id=(others[i], dom), device_id_type=MESH)

    greet(d, 1)

    def greet_dom(i, carry):
        greet(wrap(d + i, 16), 0)
        return carry

    lax.fori_loop(1, 16, greet_dom, 0)

    loads[0].wait()
    loads[1].wait()
    picks = rows[...]
    lanes16 = iota((CAP, N), 1)
    for chunk in range(8):
        hot = jnp.concatenate(
            [
                (picks[:, chunk * 16 + i : chunk * 16 + i + 1] == lanes16).astype(F32).astype(BF)
                for i in range(16)
            ],
            axis=0,
        )
        send[pl.ds(chunk * 256, 256), :] = dot(hot, xall[pl.ds(0, N), :]).astype(BF)

    pl.semaphore_wait(barrier, 127)

    up, down = wrap(d + 1, 16), wrap(d + 15, 16)
    to_up = pltpu.make_async_remote_copy(
        xall.at[pl.ds(N - HALO, HALO)], xall.at[pl.ds(N + HALO, HALO)],
        halo_s.at[0], halo_r.at[0], device_id=(g, up), device_id_type=MESH,
    )
    to_down = pltpu.make_async_remote_copy(
        xall.at[pl.ds(0, HALO)], xall.at[pl.ds(N, HALO)],
        halo_s.at[1], halo_r.at[1], device_id=(g, down), device_id_type=MESH,
    )
    to_up.start()
    to_down.start()

    tx = [wrap(x + i, 4) * 2 for i in range(4)]
    tc = [c, 1 - c]
    ty = [wrap(y + i, 4) for i in range(4)]
    tz = [wrap(z + i, 4) * 4 for i in range(4)]
    for group in range(GROUPS):
        for kz in range(4):
            for ky in range(4):
                if group + kz + ky == 0:
                    continue
                tg = tx[(group // 2 + kz + ky) % 4] + tc[group % 2]
                td = tz[kz] + ty[ky]
                pltpu.make_async_remote_copy(
                    send.at[pl.ds(pl.multiple_of((tg * 16 + td) * CAP, CAP), CAP)],
                    xall.at[pl.ds(EXP0 + group * BLK + (kz * 4 + ky) * CAP, CAP)],
                    ssem, rsem.at[group], device_id=(tg, td), device_id_type=MESH,
                ).start()
    me = g * 16 + d
    xall[pl.ds(EXP0, CAP), :] = send[pl.ds(pl.multiple_of(me * CAP, CAP), CAP), :]

    for i in range(2, 12):
        loads[i].wait()
    half = iota((BLK, 128), 1) // HD
    for r in range(0, N, BLK):
        q = (dot(xall[pl.ds(r, BLK), :], wq[...]).astype(BF) * 0.125).astype(F32)
        for h in range(H):
            pair = q[:, h // 2 * 128 : h // 2 * 128 + 128]
            qm[h, pl.ds(r, BLK), :] = jnp.where(half == h % 2, pair, 0.0).astype(BF)
    wvt[...] = wv[...].T
    vq32[...] = dot(vx[...], wq[...]).astype(BF).astype(F32) * 0.125
    vkey[...] = dot(vx[...], wk[...]).astype(BF)
    vk32[...] = vkey[...].astype(F32)
    vval = dot(vx[...], wv[...]).astype(BF)
    vv32[...] = vval.astype(F32)

    member_row = mem[...]
    member = iota((VN, N), 0) == member_row
    k_own = dot(xall[pl.ds(0, N), :], wk[...]).astype(BF)
    v_own = dot(xall[pl.ds(0, N), :], wv[...]).astype(BF)
    lane = iota((VN, 128), 1)
    part_max = jnp.zeros((VN, 128), F32)
    part_sum = jnp.zeros((VN, 128), F32)
    odd = iota((VN, 128), 1) >= HD
    scored = []
    for w in range(H // 2):
        pair = slice(w * 128, w * 128 + 128)
        vqp = vq32[:, pair]
        vqp = jnp.concatenate([jnp.where(odd, 0.0, vqp), jnp.where(odd, vqp, 0.0)], axis=0)
        scored.append(dot(vqp.astype(BF), k_own[:, pair], NT))
    parts = []
    for w in range(H // 2):
        stack = []
        for i in range(2):
            s = jnp.where(member, scored[w][i * VN : (i + 1) * VN, :], NEG)
            top = jnp.max(s, axis=1, keepdims=True)
            p = jnp.where(member, jnp.exp(s - top), 0.0)
            part_max = jnp.where(lane == 2 * w + i, top, part_max)
            part_sum = jnp.where(lane == 2 * w + i, jnp.sum(p, axis=1, keepdims=True), part_sum)
            high = p.astype(BF)
            stack += [high, (p - high.astype(F32)).astype(BF)]
        parts.append(jnp.concatenate(stack, axis=0))
    for w in range(H // 2):
        pair = slice(w * 128, w * 128 + 128)
        o = dot(parts[w], v_own[:, pair])
        even, uneven = o[:VN] + o[VN : 2 * VN], o[2 * VN : 3 * VN] + o[3 * VN :]
        part[:, pair] = jnp.where(odd, uneven, even)
    part[:, pl.ds(D, 128)] = part_max
    part[:, pl.ds(D + 128, 128)] = part_sum
    for i in range(1, 8):
        pltpu.make_async_remote_copy(
            part.at[pl.ds(pl.multiple_of(others[i] * 8, 8), 8)], r1.at[g],
            s1s, s1r, device_id=(others[i], d), device_id_type=MESH,
        ).start()
    r1[g] = part[pl.ds(pl.multiple_of(g * 8, 8), 8), :]

    win = nbr[...] - HALO
    win = jnp.where(win < 0, win + EXP0, win)
    win = jnp.where(iota((8, N), 0) < length[...], win, -1)
    for r in range(0, EXP0, 64):
        row = iota((64, N), 0) + r
        count = jnp.zeros((64, N), F32)
        for e in range(8):
            count = count + jnp.where(win[e : e + 1, :] == row, 1.0, 0.0)
        bias[pl.ds(r, 64), :] = jnp.where(count > 0.0, jnp.log(jnp.maximum(count, 1.0)), NEG)
    source = slot[...] // CAP
    sg, sd = source // 16, source % 16
    kz = (z - sd // 4 + 4) % 4
    ky = (y - sd % 4 + 4) % 4
    kc = (c - sg % 2 + 2) % 2
    kx = (x - sg // 2 + 4) % 4
    jx = (kx - kz - ky + 8) % 4
    spot = (jx * 2 + kc) * BLK + (kz * 4 + ky) * CAP + slot[...] % CAP

    def expander_bias(i, carry):
        r = pl.multiple_of(i * 64, 64)
        row = iota((64, N), 0) + r
        hit = spot[0:1, :] == row
        for e in range(1, 4):
            hit = hit | (spot[e : e + 1, :] == row)
        bias[pl.ds(EXP0 + r, 64), :] = jnp.where(hit, 0.0, NEG)
        return carry

    lax.fori_loop(0, GROUPS * BLK // 64, expander_bias, 0)

    vvt = vval.T
    vbias[...] = jnp.where(member, 0.0, NEG)
    for h in range(H):
        pair = slice(h // 2 * 128, h // 2 * 128 + 128)
        s = dot(vkey[:, pair], qm[h], NT) + vbias[...]
        top = jnp.max(s, axis=0, keepdims=True)
        m_ref[h : h + 1, :] = top
        p = jnp.exp((s - top).astype(BF))
        vals = jnp.concatenate([vvt[h * HD : (h + 1) * HD, :], jnp.ones((VR - HD, VN), BF)], axis=0)
        acc[h] = dot(vals, p)[:AR, :]
        vt[h, pl.ds(HD, VR - HD), :] = jnp.ones((VR - HD, BLK), BF)

    def wait_bytes(like, sem):
        pltpu.make_async_copy(like, like, sem).wait()

    expand = expander(128)

    def combine(parts):
        tops = [q[:, D : D + 128] for q in parts]
        top = functools.reduce(jnp.maximum, tops)
        scale = [jnp.exp(t - top) for t in tops]
        total = functools.reduce(jnp.add, [q[:, D + 128 :] * f for q, f in zip(parts, scale)])
        wide = dot(jnp.concatenate(scale, axis=0), expand, precision=lax.Precision.HIGHEST)
        n = parts[0].shape[0]
        mixed = functools.reduce(
            jnp.add, [q[:, :D] * wide[i * n : (i + 1) * n, :] for i, q in enumerate(parts)]
        )
        return mixed, top, total

    def block(b, carry):
        @pl.when(b == OWN_BLOCKS)
        def _():
            to_up.wait_recv()
            to_down.wait_recv()

        @pl.when(b == FIRST_EXP)
        def _():
            wait_bytes(xall.at[pl.ds(EXP0, 15 * CAP)], rsem.at[0])

        @pl.when(b > FIRST_EXP)
        def _():
            wait_bytes(xall.at[pl.ds(EXP0, 16 * CAP)], rsem.at[b - FIRST_EXP])

        @pl.when(b == FIRST_EXP)
        def _():
            wait_bytes(r1.at[pl.ds(0, 7)], s1r)
            mixed, top, total = combine([r1[i] for i in range(8)])
            for i in range(8):
                c1[i, :, pl.ds(0, D)] = mixed[i : i + 1, :]
                c1[i, :, pl.ds(D, 128)] = top[i : i + 1, :]
                c1[i, :, pl.ds(D + 128, 128)] = total[i : i + 1, :]

            for i in range(8):
                @pl.when(d != i)
                def _():
                    pltpu.make_async_remote_copy(
                        c1.at[i], r2.at[d], s2s, s2r, device_id=(g, i), device_id_type=MESH
                    ).start()

            @pl.when(d < 8)
            def _():
                r2[d] = c1[d]

        @pl.when((b == FIRST_EXP + 2) & (d < 8))
        def _():
            wait_bytes(r2.at[pl.ds(0, 15)], s2r)
            mixed, top, total = combine([r2[i] for i in range(16)])
            v = g * 8 + d
            vq, vk, vv = vq32[pl.ds(v, 1), :], vk32[pl.ds(v, 1), :], vv32[pl.ds(v, 1), :]
            eight = lambda row: jnp.broadcast_to(row, (8, row.shape[1]))
            own = dot(eight(vq * vk), expand, NT, precision=lax.Precision.HIGHEST)[0:1, :]
            peak = jnp.maximum(top, own)
            old, new = jnp.exp(top - peak), jnp.exp(own - peak)
            denom = total * old + new
            factors = jnp.concatenate([old, new, denom], axis=0)
            factors = jnp.concatenate([factors, jnp.zeros((5, 128), F32)], axis=0)
            wide = dot(factors, expand, precision=lax.Precision.HIGHEST)
            va = (mixed * wide[0:1, :] + wide[1:2, :] * vv) / wide[2:3, :]
            proj = dot(eight(va).astype(BF), wo[...])
            u = eight(vx_row(v)) + proj
            vrow[0] = norm(u, ga[...]).astype(BF).astype(F32)[0:1, :]
            for i in range(1, 16):
                pltpu.make_async_remote_copy(
                    vrow.at[0], r3a.at[d], s3s, s3r,
                    device_id=(g, wrap(d + i, 16)), device_id_type=MESH,
                ).start()
            r3a[d] = vrow[0]

        @pl.when(b == FIRST_EXP + 5)
        def _():
            @pl.when(d < 8)
            def _():
                wait_bytes(r3a.at[pl.ds(0, 7)], s3r)

            @pl.when(d >= 8)
            def _():
                wait_bytes(r3a.at[pl.ds(0, 8)], s3r)

            r3[g] = r3a[:, 0, :]
            for i in range(1, 8):
                pltpu.make_async_remote_copy(
                    r3.at[g], r3.at[g], s4s, s4r, device_id=(others[i], d), device_id_type=MESH
                ).start()

        r = pl.multiple_of(b * BLK, BLK)
        xb = xall[pl.ds(r, BLK), :]
        kblk[...] = dot(xb, wk[...]).astype(BF)
        vals = dot(wvt[...], xb, NT).astype(BF)
        for h in range(H):
            vt[h, pl.ds(0, HD), :] = vals[h * HD : (h + 1) * HD, :]
        add = bias[pl.ds(r, BLK), :]
        scored = [dot(kblk[:, h // 2 * 128 : h // 2 * 128 + 128], qm[h], NT) for h in range(H)]
        weighed = []
        for h in range(H):
            s = scored[h] + add
            old = m_ref[h : h + 1, :]
            top = jnp.maximum(old, jnp.max(s, axis=0, keepdims=True))
            m_ref[h : h + 1, :] = top
            weighed.append((jnp.exp((s - top).astype(BF)), jnp.exp(old - top)))
        for h in range(H):
            p, keep = weighed[h]
            acc[h] = acc[h] * keep + dot(vt[h], p)[:AR, :]
        return carry

    def vx_row(v):
        return vx32_row(vx, v)

    loads[12].wait()
    lax.fori_loop(0, BLOCKS, block, 0)

    for h in range(H):
        span = slice(h * HD, (h + 1) * HD)
        att[span, :] = (acc[h, :HD, :] * (1.0 / acc[h, HD : HD + 1, :])).astype(BF)
    loads[13].wait()
    loads[14].wait()
    attn = att[...].T
    att[...] = attn
    for r in range(0, N, BLK):
        at = pl.ds(r, BLK)
        mixed = xall[at, :].astype(F32) + dot(att[at, :], wo[...])
        settled = norm(mixed, ga[...]).astype(BF)
        total = settled.astype(F32)
        for f in range(0, 4 * D, D):
            hidden = jnp.maximum(dot(settled, wu[:, f : f + D]), 0.0).astype(BF)
            total = total + dot(hidden, wd[f : f + D, :])
        outs[at, :] = norm(total, gf[...]).astype(BF)
        pltpu.make_async_copy(outs.at[at], out_hbm.at[at], out_sem.at[r // BLK]).start()

    wait_bytes(r3.at[pl.ds(0, 7)], s4r)
    vout[...] = r3[...].reshape(VN, D).astype(BF)
    last = pltpu.make_async_copy(vout, vout_hbm, out_sem.at[2])
    last.start()

    to_up.wait_send()
    to_down.wait_send()
    wait_bytes(send.at[pl.ds(0, 127 * CAP)], ssem)
    wait_bytes(part.at[pl.ds(0, 56)], s1s)

    @pl.when(d < 8)
    def _():
        wait_bytes(c1.at[pl.ds(0, 7)], s2s)
        wait_bytes(r2.at[pl.ds(0, 15), :, pl.ds(0, D)], s3s)

    @pl.when(d >= 8)
    def _():
        wait_bytes(c1, s2s)

    wait_bytes(r3.at[pl.ds(0, 7)], s4s)
    for r in range(0, N, BLK):
        at = pl.ds(r, BLK)
        pltpu.make_async_copy(outs.at[at], out_hbm.at[at], out_sem.at[r // BLK]).wait()
    last.wait()


def vx32_row(vx, v):
    hot = (iota((8, VN), 1) == v).astype(F32).astype(BF)
    return dot(hot, vx[...])[0:1, :]


def hand_over(node, virtual, node_out, virtual_out, sem):
    copies = [pltpu.make_async_copy(virtual, virtual_out, sem.at[4])]
    for i in range(4):
        at = pl.ds(i * 128, 128)
        copies.append(pltpu.make_async_copy(node.at[at], node_out.at[at], sem.at[i]))
    for copy in copies:
        copy.start()
    for copy in copies:
        copy.wait()


def shards(
    node_input, virtual_input, w_query, w_key, w_value, w_out, w_up, w_down, gain_attn, gain_ffn,
    local_nbr, local_len, send_rows, exp_slot, membership,
):
    args = (
        node_input, virtual_input, w_query, w_key, w_value, w_out, w_up, w_down,
        gain_attn.reshape(1, D), gain_ffn.reshape(1, D), local_nbr.T, local_len.reshape(1, N),
        send_rows[0].T, exp_slot.T, membership.reshape(1, N),
    )
    vmem = pltpu.VMEM
    dma = pltpu.SemaphoreType.DMA
    scratch = [
        vmem((ROWS, D), BF), vmem((VN, D), BF), vmem((D, D), BF), vmem((D, D), BF),
        vmem((D, D), BF), vmem((D, D), BF), vmem((D, 4 * D), BF), vmem((4 * D, D), BF),
        vmem((1, D), F32), vmem((1, D), F32), vmem((8, N), jnp.int32), vmem((1, N), jnp.int32),
        vmem((CAP, 128), jnp.int32), vmem((4, N), jnp.int32), vmem((1, N), jnp.int32),
        vmem((128 * CAP, D), BF), vmem((D, D), BF), vmem((H, N, 128), BF), vmem((ROWS, N), F32),
        vmem((BLK, D), BF), vmem((H, VR, BLK), BF), vmem((H, N), F32),
        vmem((H, AR, N), F32), vmem((D, N), BF), vmem((N, D), BF),
        vmem((VN, D), F32), vmem((VN, D), F32), vmem((VN, D), F32), vmem((VN, D), BF),
        vmem((VN, N), F32), vmem((VN, PART), F32), vmem((8, 8, PART), F32),
        vmem((8, 1, PART), F32), vmem((16, 1, PART), F32), vmem((8, 1, D), F32),
        vmem((8, 8, D), F32), vmem((1, 1, D), F32), vmem((VN, D), BF),
        dma((15,)), dma((3,)), dma, dma((GROUPS,)), dma((2,)), dma((2,)),
        dma, dma, dma, dma, dma, dma, dma, dma,
    ]
    hbm = pl.BlockSpec(memory_space=pl.ANY)
    node, virtual = pl.pallas_call(
        kernel,
        out_shape=(
            jax.ShapeDtypeStruct((N, D), BF),
            jax.ShapeDtypeStruct((VN, D), BF),
        ),
        in_specs=[hbm] * len(args),
        out_specs=(hbm, hbm),
        scratch_shapes=scratch,
        compiler_params=pltpu.CompilerParams(
            collective_id=0, has_side_effects=True, vmem_limit_bytes=56 * 1024 * 1024
        ),
    )(*args)
    return pl.pallas_call(
        hand_over,
        out_shape=(
            jax.ShapeDtypeStruct((N, D), BF),
            jax.ShapeDtypeStruct((VN, D), BF),
        ),
        in_specs=[hbm] * 2,
        out_specs=(hbm, hbm),
        scratch_shapes=[dma((5,))],
        compiler_params=pltpu.CompilerParams(vmem_limit_bytes=60 * 1024 * 1024),
    )(node, virtual)


def solution(mesh):
    rows = P(("group", "dom"), None)
    line = P(("group", "dom"))
    placed = (
        rows, P(), P(), P(), P(), P(), P(), P(), P(), P(),
        rows, line, P(("group", "dom"), None, None), rows, line,
    )
    return jax.shard_map(
        shards, mesh=mesh, in_specs=placed, out_specs=(rows, P()), check_vma=False
    )
```

```python
import functools

import jax
import jax.numpy as jnp
from jax import lax
from jax.experimental import pallas as pl
from jax.experimental.pallas import tpu as pltpu
from jax.sharding import PartitionSpec as P

MESH = pl.DeviceIdType.MESH
BF = jnp.bfloat16
F32 = jnp.float32
NEG = -1e30

D = 512
H = 8
HD = D // H
N = 512
VN = 64
HALO = 128
CAP = 16
BLK = 256
OWN_BLOCKS = N // BLK
FIRST_EXP = OWN_BLOCKS + 1
GROUPS = 8
BLOCKS = FIRST_EXP + GROUPS
ROWS = BLOCKS * BLK
EXP0 = FIRST_EXP * BLK
PART = D + 256
VR = HD + 16
AR = HD + 8


def dot(a, b, dims=((1,), (0,)), precision=None):
    return lax.dot_general(a, b, (dims, ((), ())), precision=precision, preferred_element_type=F32)


NT = ((1,), (1,))


def iota(shape, dim):
    return lax.broadcasted_iota(jnp.int32, shape, dim)


def norm(u, gain):
    center = u - jnp.mean(u, axis=-1, keepdims=True)
    spread = jnp.mean(center * center, axis=-1, keepdims=True)
    return center * lax.rsqrt(spread + 1e-05) * gain


def expander(rows):
    return (iota((rows, D), 1) // HD == iota((rows, D), 0)).astype(F32)


def wrap(value, size):
    return jnp.where(value >= size, value - size, value)


def kernel(
    x_hbm, vx_hbm, wq_hbm, wk_hbm, wv_hbm, wo_hbm, wu_hbm, wd_hbm, ga_hbm, gf_hbm,
    nbr_hbm, len_hbm, rows_hbm, slot_hbm, mem_hbm,
    out_hbm, vout_hbm,
    xall, vx, wq, wk, wv, wo, wu, wd, ga, gf, nbr, length, rows, slot, mem,
    send, wvt, qm, bias, kblk, vt, m_ref, acc, att, outs,
    vq32, vk32, vv32, vkey, vbias, part, r1, c1, r2, r3a, r3, vrow, vout,
    in_sem, out_sem, ssem, rsem, halo_s, halo_r, s1s, s1r, s2s, s2r, s3s, s3r, s4s, s4r,
):
    g = lax.axis_index("group")
    d = lax.axis_index("dom")
    x, c = g // 2, g % 2
    z, y = d // 4, d % 4

    order = [
        (x_hbm, xall.at[pl.ds(0, N)]), (rows_hbm, rows), (wq_hbm, wq), (wk_hbm, wk), (wv_hbm, wv),
        (vx_hbm, vx), (mem_hbm, mem), (len_hbm, length), (nbr_hbm, nbr), (slot_hbm, slot),
        (ga_hbm, ga), (gf_hbm, gf), (wo_hbm, wo), (wu_hbm, wu), (wd_hbm, wd),
    ]
    loads = [pltpu.make_async_copy(a, b, in_sem.at[i]) for i, (a, b) in enumerate(order)]
    for load in loads:
        load.start()

    barrier = pltpu.get_barrier_semaphore()
    others = [wrap(g + i, H) for i in range(8)]

    def greet(dom, first):
        for i in range(first, 8):
            pl.semaphore_signal(barrier, inc=1, device_id=(others[i], dom), device_id_type=MESH)

    greet(d, 1)

    def greet_dom(i, carry):
        greet(wrap(d + i, 16), 0)
        return carry

    lax.fori_loop(1, 16, greet_dom, 0)

    loads[0].wait()
    loads[1].wait()
    picks = rows[...]
    lanes16 = iota((CAP, N), 1)
    for chunk in range(8):
        hot = jnp.concatenate(
            [
                (picks[:, chunk * 16 + i : chunk * 16 + i + 1] == lanes16).astype(F32).astype(BF)
                for i in range(16)
            ],
            axis=0,
        )
        send[pl.ds(chunk * 256, 256), :] = dot(hot, xall[pl.ds(0, N), :]).astype(BF)

    pl.semaphore_wait(barrier, 127)

    up, down = wrap(d + 1, 16), wrap(d + 15, 16)
    to_up = pltpu.make_async_remote_copy(
        xall.at[pl.ds(N - HALO, HALO)], xall.at[pl.ds(N + HALO, HALO)],
        halo_s.at[0], halo_r.at[0], device_id=(g, up), device_id_type=MESH,
    )
    to_down = pltpu.make_async_remote_copy(
        xall.at[pl.ds(0, HALO)], xall.at[pl.ds(N, HALO)],
        halo_s.at[1], halo_r.at[1], device_id=(g, down), device_id_type=MESH,
    )
    to_up.start()
    to_down.start()

    tx = [wrap(x + i, 4) * 2 for i in range(4)]
    tc = [c, 1 - c]
    ty = [wrap(y + i, 4) for i in range(4)]
    tz = [wrap(z + i, 4) * 4 for i in range(4)]
    for group in range(GROUPS):
        for kz in range(4):
            for ky in range(4):
                if group + kz + ky == 0:
                    continue
                tg = tx[(group // 2 + kz + ky) % 4] + tc[group % 2]
                td = tz[kz] + ty[ky]
                pltpu.make_async_remote_copy(
                    send.at[pl.ds(pl.multiple_of((tg * 16 + td) * CAP, CAP), CAP)],
                    xall.at[pl.ds(EXP0 + group * BLK + (kz * 4 + ky) * CAP, CAP)],
                    ssem, rsem.at[group], device_id=(tg, td), device_id_type=MESH,
                ).start()
    me = g * 16 + d
    xall[pl.ds(EXP0, CAP), :] = send[pl.ds(pl.multiple_of(me * CAP, CAP), CAP), :]

    for i in range(2, 12):
        loads[i].wait()
    half = iota((BLK, 128), 1) // HD
    for r in range(0, N, BLK):
        q = (dot(xall[pl.ds(r, BLK), :], wq[...]).astype(BF) * 0.125).astype(F32)
        for h in range(H):
            pair = q[:, h // 2 * 128 : h // 2 * 128 + 128]
            qm[h, pl.ds(r, BLK), :] = jnp.where(half == h % 2, pair, 0.0).astype(BF)
    wvt[...] = wv[...].T
    vq32[...] = dot(vx[...], wq[...]).astype(BF).astype(F32) * 0.125
    vkey[...] = dot(vx[...], wk[...]).astype(BF)
    vk32[...] = vkey[...].astype(F32)
    vval = dot(vx[...], wv[...]).astype(BF)
    vv32[...] = vval.astype(F32)

    member_row = mem[...]
    member = iota((VN, N), 0) == member_row
    k_own = dot(xall[pl.ds(0, N), :], wk[...]).astype(BF)
    v_own = dot(xall[pl.ds(0, N), :], wv[...]).astype(BF)
    lane = iota((VN, 128), 1)
    part_max = jnp.zeros((VN, 128), F32)
    part_sum = jnp.zeros((VN, 128), F32)
    odd = iota((VN, 128), 1) >= HD
    scored = []
    for w in range(H // 2):
        pair = slice(w * 128, w * 128 + 128)
        vqp = vq32[:, pair]
        vqp = jnp.concatenate([jnp.where(odd, 0.0, vqp), jnp.where(odd, vqp, 0.0)], axis=0)
        scored.append(dot(vqp.astype(BF), k_own[:, pair], NT))
    parts = []
    for w in range(H // 2):
        stack = []
        for i in range(2):
            s = jnp.where(member, scored[w][i * VN : (i + 1) * VN, :], NEG)
            top = jnp.max(s, axis=1, keepdims=True)
            p = jnp.where(member, jnp.exp(s - top), 0.0)
            part_max = jnp.where(lane == 2 * w + i, top, part_max)
            part_sum = jnp.where(lane == 2 * w + i, jnp.sum(p, axis=1, keepdims=True), part_sum)
            high = p.astype(BF)
            stack += [high, (p - high.astype(F32)).astype(BF)]
        parts.append(jnp.concatenate(stack, axis=0))
    for w in range(H // 2):
        pair = slice(w * 128, w * 128 + 128)
        o = dot(parts[w], v_own[:, pair])
        even, uneven = o[:VN] + o[VN : 2 * VN], o[2 * VN : 3 * VN] + o[3 * VN :]
        part[:, pair] = jnp.where(odd, uneven, even)
    part[:, pl.ds(D, 128)] = part_max
    part[:, pl.ds(D + 128, 128)] = part_sum
    for i in range(1, 8):
        pltpu.make_async_remote_copy(
            part.at[pl.ds(pl.multiple_of(others[i] * 8, 8), 8)], r1.at[g],
            s1s, s1r, device_id=(others[i], d), device_id_type=MESH,
        ).start()
    r1[g] = part[pl.ds(pl.multiple_of(g * 8, 8), 8), :]

    win = nbr[...] - HALO
    win = jnp.where(win < 0, win + EXP0, win)
    win = jnp.where(iota((8, N), 0) < length[...], win, -1)
    for r in range(0, EXP0, 64):
        row = iota((64, N), 0) + r
        count = jnp.zeros((64, N), F32)
        for e in range(8):
            count = count + jnp.where(win[e : e + 1, :] == row, 1.0, 0.0)
        bias[pl.ds(r, 64), :] = jnp.where(count > 0.0, jnp.log(jnp.maximum(count, 1.0)), NEG)
    source = slot[...] // CAP
    sg, sd = source // 16, source % 16
    kz = (z - sd // 4 + 4) % 4
    ky = (y - sd % 4 + 4) % 4
    kc = (c - sg % 2 + 2) % 2
    kx = (x - sg // 2 + 4) % 4
    jx = (kx - kz - ky + 8) % 4
    spot = (jx * 2 + kc) * BLK + (kz * 4 + ky) * CAP + slot[...] % CAP

    def expander_bias(i, carry):
        r = pl.multiple_of(i * 64, 64)
        row = iota((64, N), 0) + r
        hit = spot[0:1, :] == row
        for e in range(1, 4):
            hit = hit | (spot[e : e + 1, :] == row)
        bias[pl.ds(EXP0 + r, 64), :] = jnp.where(hit, 0.0, NEG)
        return carry

    lax.fori_loop(0, GROUPS * BLK // 64, expander_bias, 0)

    vvt = vval.T
    vbias[...] = jnp.where(member, 0.0, NEG)
    for h in range(H):
        pair = slice(h // 2 * 128, h // 2 * 128 + 128)
        s = dot(vkey[:, pair], qm[h], NT) + vbias[...]
        top = jnp.max(s, axis=0, keepdims=True)
        m_ref[h : h + 1, :] = top
        p = jnp.exp((s - top).astype(BF))
        vals = jnp.concatenate([vvt[h * HD : (h + 1) * HD, :], jnp.ones((VR - HD, VN), BF)], axis=0)
        acc[h] = dot(vals, p)[:AR, :]
        vt[h, pl.ds(HD, VR - HD), :] = jnp.ones((VR - HD, BLK), BF)

    def wait_bytes(like, sem):
        pltpu.make_async_copy(like, like, sem).wait()

    expand = expander(128)

    def combine(parts):
        tops = [q[:, D : D + 128] for q in parts]
        top = functools.reduce(jnp.maximum, tops)
        scale = [jnp.exp(t - top) for t in tops]
        total = functools.reduce(jnp.add, [q[:, D + 128 :] * f for q, f in zip(parts, scale)])
        wide = dot(jnp.concatenate(scale, axis=0), expand, precision=lax.Precision.HIGHEST)
        n = parts[0].shape[0]
        mixed = functools.reduce(
            jnp.add, [q[:, :D] * wide[i * n : (i + 1) * n, :] for i, q in enumerate(parts)]
        )
        return mixed, top, total

    def block(b, carry):
        @pl.when(b == OWN_BLOCKS)
        def _():
            to_up.wait_recv()
            to_down.wait_recv()

        @pl.when(b == FIRST_EXP)
        def _():
            wait_bytes(xall.at[pl.ds(EXP0, 15 * CAP)], rsem.at[0])

        @pl.when(b > FIRST_EXP)
        def _():
            wait_bytes(xall.at[pl.ds(EXP0, 16 * CAP)], rsem.at[b - FIRST_EXP])

        @pl.when(b == FIRST_EXP)
        def _():
            wait_bytes(r1.at[pl.ds(0, 7)], s1r)
            mixed, top, total = combine([r1[i] for i in range(8)])
            for i in range(8):
                c1[i, :, pl.ds(0, D)] = mixed[i : i + 1, :]
                c1[i, :, pl.ds(D, 128)] = top[i : i + 1, :]
                c1[i, :, pl.ds(D + 128, 128)] = total[i : i + 1, :]

            for i in range(8):
                @pl.when(d != i)
                def _():
                    pltpu.make_async_remote_copy(
                        c1.at[i], r2.at[d], s2s, s2r, device_id=(g, i), device_id_type=MESH
                    ).start()

            @pl.when(d < 8)
            def _():
                r2[d] = c1[d]

        @pl.when((b == FIRST_EXP + 2) & (d < 8))
        def _():
            wait_bytes(r2.at[pl.ds(0, 15)], s2r)
            mixed, top, total = combine([r2[i] for i in range(16)])
            v = g * 8 + d
            vq, vk, vv = vq32[pl.ds(v, 1), :], vk32[pl.ds(v, 1), :], vv32[pl.ds(v, 1), :]
            eight = lambda row: jnp.broadcast_to(row, (8, row.shape[1]))
            own = dot(eight(vq * vk), expand, NT, precision=lax.Precision.HIGHEST)[0:1, :]
            peak = jnp.maximum(top, own)
            old, new = jnp.exp(top - peak), jnp.exp(own - peak)
            denom = total * old + new
            factors = jnp.concatenate([old, new, denom], axis=0)
            factors = jnp.concatenate([factors, jnp.zeros((5, 128), F32)], axis=0)
            wide = dot(factors, expand, precision=lax.Precision.HIGHEST)
            va = (mixed * wide[0:1, :] + wide[1:2, :] * vv) / wide[2:3, :]
            proj = dot(eight(va).astype(BF), wo[...])
            u = eight(vx_row(v)) + proj
            vrow[0] = norm(u, ga[...]).astype(BF).astype(F32)[0:1, :]
            for i in range(1, 16):
                pltpu.make_async_remote_copy(
                    vrow.at[0], r3a.at[d], s3s, s3r,
                    device_id=(g, wrap(d + i, 16)), device_id_type=MESH,
                ).start()
            r3a[d] = vrow[0]

        @pl.when(b == FIRST_EXP + 5)
        def _():
            @pl.when(d < 8)
            def _():
                wait_bytes(r3a.at[pl.ds(0, 7)], s3r)

            @pl.when(d >= 8)
            def _():
                wait_bytes(r3a.at[pl.ds(0, 8)], s3r)

            r3[g] = r3a[:, 0, :]
            for i in range(1, 8):
                pltpu.make_async_remote_copy(
                    r3.at[g], r3.at[g], s4s, s4r, device_id=(others[i], d), device_id_type=MESH
                ).start()

        r = pl.multiple_of(b * BLK, BLK)
        xb = xall[pl.ds(r, BLK), :]
        kblk[...] = dot(xb, wk[...]).astype(BF)
        vals = dot(wvt[...], xb, NT).astype(BF)
        for h in range(H):
            vt[h, pl.ds(0, HD), :] = vals[h * HD : (h + 1) * HD, :]
        add = bias[pl.ds(r, BLK), :]
        scored = [dot(kblk[:, h // 2 * 128 : h // 2 * 128 + 128], qm[h], NT) for h in range(H)]
        weighed = []
        for h in range(H):
            s = scored[h] + add
            old = m_ref[h : h + 1, :]
            top = jnp.maximum(old, jnp.max(s, axis=0, keepdims=True))
            m_ref[h : h + 1, :] = top
            weighed.append((jnp.exp((s - top).astype(BF)), jnp.exp(old - top)))
        for h in range(H):
            p, keep = weighed[h]
            acc[h] = acc[h] * keep + dot(vt[h], p)[:AR, :]
        return carry

    def vx_row(v):
        return vx32_row(vx, v)

    loads[12].wait()
    lax.fori_loop(0, BLOCKS, block, 0)

    for h in range(H):
        span = slice(h * HD, (h + 1) * HD)
        att[span, :] = (acc[h, :HD, :] * (1.0 / acc[h, HD : HD + 1, :])).astype(BF)
    loads[13].wait()
    loads[14].wait()
    attn = att[...].T
    att[...] = attn
    for r in range(0, N, BLK):
        at = pl.ds(r, BLK)
        mixed = xall[at, :].astype(F32) + dot(att[at, :], wo[...])
        settled = norm(mixed, ga[...]).astype(BF)
        total = settled.astype(F32)
        for f in range(0, 4 * D, D):
            hidden = jnp.maximum(dot(settled, wu[:, f : f + D]), 0.0).astype(BF)
            total = total + dot(hidden, wd[f : f + D, :])
        outs[at, :] = norm(total, gf[...]).astype(BF)
        pltpu.make_async_copy(outs.at[at], out_hbm.at[at], out_sem.at[r // BLK]).start()

    wait_bytes(r3.at[pl.ds(0, 7)], s4r)
    vout[...] = r3[...].reshape(VN, D).astype(BF)
    last = pltpu.make_async_copy(vout, vout_hbm, out_sem.at[2])
    last.start()

    to_up.wait_send()
    to_down.wait_send()
    wait_bytes(send.at[pl.ds(0, 127 * CAP)], ssem)
    wait_bytes(part.at[pl.ds(0, 56)], s1s)

    @pl.when(d < 8)
    def _():
        wait_bytes(c1.at[pl.ds(0, 7)], s2s)
        wait_bytes(r2.at[pl.ds(0, 15), :, pl.ds(0, D)], s3s)

    @pl.when(d >= 8)
    def _():
        wait_bytes(c1, s2s)

    wait_bytes(r3.at[pl.ds(0, 7)], s4s)
    for r in range(0, N, BLK):
        at = pl.ds(r, BLK)
        pltpu.make_async_copy(outs.at[at], out_hbm.at[at], out_sem.at[r // BLK]).wait()
    last.wait()


def vx32_row(vx, v):
    hot = (iota((8, VN), 1) == v).astype(F32).astype(BF)
    return dot(hot, vx[...])[0:1, :]


def hand_over(node, virtual, node_out, virtual_out, held, vheld, sem):
    steps = [(virtual, vheld, virtual_out)]
    for i in range(4):
        at = pl.ds(i * 128, 128)
        steps.append((node.at[at], held.at[at], node_out.at[at]))
    loads = [pltpu.make_async_copy(a, b, sem.at[0, i]) for i, (a, b, _) in enumerate(steps)]
    stores = [pltpu.make_async_copy(b, c, sem.at[1, i]) for i, (_, b, c) in enumerate(steps)]
    for load in loads:
        load.start()
    for load, store in zip(loads, stores):
        load.wait()
        store.start()
    for store in stores:
        store.wait()


def shards(
    node_input, virtual_input, w_query, w_key, w_value, w_out, w_up, w_down, gain_attn, gain_ffn,
    local_nbr, local_len, send_rows, exp_slot, membership,
):
    args = (
        node_input, virtual_input, w_query, w_key, w_value, w_out, w_up, w_down,
        gain_attn.reshape(1, D), gain_ffn.reshape(1, D), local_nbr.T, local_len.reshape(1, N),
        send_rows[0].T, exp_slot.T, membership.reshape(1, N),
    )
    vmem = pltpu.VMEM
    dma = pltpu.SemaphoreType.DMA
    scratch = [
        vmem((ROWS, D), BF), vmem((VN, D), BF), vmem((D, D), BF), vmem((D, D), BF),
        vmem((D, D), BF), vmem((D, D), BF), vmem((D, 4 * D), BF), vmem((4 * D, D), BF),
        vmem((1, D), F32), vmem((1, D), F32), vmem((8, N), jnp.int32), vmem((1, N), jnp.int32),
        vmem((CAP, 128), jnp.int32), vmem((4, N), jnp.int32), vmem((1, N), jnp.int32),
        vmem((128 * CAP, D), BF), vmem((D, D), BF), vmem((H, N, 128), BF), vmem((ROWS, N), F32),
        vmem((BLK, D), BF), vmem((H, VR, BLK), BF), vmem((H, N), F32),
        vmem((H, AR, N), F32), vmem((D, N), BF), vmem((N, D), BF),
        vmem((VN, D), F32), vmem((VN, D), F32), vmem((VN, D), F32), vmem((VN, D), BF),
        vmem((VN, N), F32), vmem((VN, PART), F32), vmem((8, 8, PART), F32),
        vmem((8, 1, PART), F32), vmem((16, 1, PART), F32), vmem((8, 1, D), F32),
        vmem((8, 8, D), F32), vmem((1, 1, D), F32), vmem((VN, D), BF),
        dma((15,)), dma((3,)), dma, dma((GROUPS,)), dma((2,)), dma((2,)),
        dma, dma, dma, dma, dma, dma, dma, dma,
    ]
    hbm = pl.BlockSpec(memory_space=pl.ANY)
    node, virtual = pl.pallas_call(
        kernel,
        out_shape=(
            jax.ShapeDtypeStruct((N, D), BF),
            jax.ShapeDtypeStruct((VN, D), BF),
        ),
        in_specs=[hbm] * len(args),
        out_specs=(hbm, hbm),
        scratch_shapes=scratch,
        compiler_params=pltpu.CompilerParams(
            collective_id=0, has_side_effects=True, vmem_limit_bytes=56 * 1024 * 1024
        ),
    )(*args)
    return pl.pallas_call(
        hand_over,
        out_shape=(
            jax.ShapeDtypeStruct((N, D), BF),
            jax.ShapeDtypeStruct((VN, D), BF),
        ),
        in_specs=[hbm] * 2,
        out_specs=(hbm, hbm),
        scratch_shapes=[vmem((N, D), BF), vmem((VN, D), BF), dma((2, 5))],
        compiler_params=pltpu.CompilerParams(vmem_limit_bytes=60 * 1024 * 1024),
    )(node, virtual)


def solution(mesh):
    rows = P(("group", "dom"), None)
    line = P(("group", "dom"))
    placed = (
        rows, P(), P(), P(), P(), P(), P(), P(), P(), P(),
        rows, line, P(("group", "dom"), None, None), rows, line,
    )
    return jax.shard_map(
        shards, mesh=mesh, in_specs=placed, out_specs=(rows, P()), check_vma=False
    )
```

```python
import functools

import jax
import jax.numpy as jnp
from jax import lax
from jax.experimental import pallas as pl
from jax.experimental.pallas import tpu as pltpu
from jax.sharding import PartitionSpec as P

MESH = pl.DeviceIdType.MESH
BF = jnp.bfloat16
F32 = jnp.float32
NEG = -1e30

D = 512
H = 8
HD = D // H
N = 512
VN = 64
HALO = 128
CAP = 16
BLK = 256
OWN_BLOCKS = N // BLK
FIRST_EXP = OWN_BLOCKS + 1
GROUPS = 8
BLOCKS = FIRST_EXP + GROUPS
ROWS = BLOCKS * BLK
EXP0 = FIRST_EXP * BLK
PART = D + 256
VR = HD + 16
AR = HD + 8


def dot(a, b, dims=((1,), (0,)), precision=None):
    return lax.dot_general(a, b, (dims, ((), ())), precision=precision, preferred_element_type=F32)


NT = ((1,), (1,))


def iota(shape, dim):
    return lax.broadcasted_iota(jnp.int32, shape, dim)


def norm(u, gain):
    center = u - jnp.mean(u, axis=-1, keepdims=True)
    spread = jnp.mean(center * center, axis=-1, keepdims=True)
    return center * lax.rsqrt(spread + 1e-05) * gain


def expander(rows):
    return (iota((rows, D), 1) // HD == iota((rows, D), 0)).astype(F32)


def wrap(value, size):
    return jnp.where(value >= size, value - size, value)


def kernel(
    x_hbm, vx_hbm, wq_hbm, wk_hbm, wv_hbm, wo_hbm, wu_hbm, wd_hbm, ga_hbm, gf_hbm,
    nbr_hbm, len_hbm, rows_hbm, slot_hbm, mem_hbm,
    out_hbm, vout_hbm,
    xall, vx, wq, wk, wv, wo, wu, wd, ga, gf, nbr, length, rows, slot, mem,
    send, wvt, qm, bias, kblk, vt, m_ref, acc, att, outs,
    vq32, vk32, vv32, vkey, vbias, part, r1, c1, r2, r3a, r3, vrow, vout,
    in_sem, out_sem, ssem, rsem, halo_s, halo_r, s1s, s1r, s2s, s2r, s3s, s3r, s4s, s4r,
):
    g = lax.axis_index("group")
    d = lax.axis_index("dom")
    x, c = g // 2, g % 2
    z, y = d // 4, d % 4

    order = [
        (x_hbm, xall.at[pl.ds(0, N)]), (rows_hbm, rows), (wq_hbm, wq), (wk_hbm, wk), (wv_hbm, wv),
        (vx_hbm, vx), (mem_hbm, mem), (len_hbm, length), (nbr_hbm, nbr), (slot_hbm, slot),
        (ga_hbm, ga), (gf_hbm, gf), (wo_hbm, wo), (wu_hbm, wu), (wd_hbm, wd),
    ]
    loads = [pltpu.make_async_copy(a, b, in_sem.at[i]) for i, (a, b) in enumerate(order)]
    for load in loads:
        load.start()

    barrier = pltpu.get_barrier_semaphore()
    others = [wrap(g + i, H) for i in range(8)]

    def greet(dom, first):
        for i in range(first, 8):
            pl.semaphore_signal(barrier, inc=1, device_id=(others[i], dom), device_id_type=MESH)

    greet(d, 1)

    def greet_dom(i, carry):
        greet(wrap(d + i, 16), 0)
        return carry

    lax.fori_loop(1, 16, greet_dom, 0)

    loads[0].wait()
    loads[1].wait()
    picks = rows[...]
    lanes16 = iota((CAP, N), 1)
    for chunk in range(8):
        hot = jnp.concatenate(
            [
                (picks[:, chunk * 16 + i : chunk * 16 + i + 1] == lanes16).astype(F32).astype(BF)
                for i in range(16)
            ],
            axis=0,
        )
        send[pl.ds(chunk * 256, 256), :] = dot(hot, xall[pl.ds(0, N), :]).astype(BF)

    for i in range(2, 12):
        loads[i].wait()
    half = iota((BLK, 128), 1) // HD
    for r in range(0, N, BLK):
        q = (dot(xall[pl.ds(r, BLK), :], wq[...]).astype(BF) * 0.125).astype(F32)
        for h in range(H):
            pair = q[:, h // 2 * 128 : h // 2 * 128 + 128]
            qm[h, pl.ds(r, BLK), :] = jnp.where(half == h % 2, pair, 0.0).astype(BF)
    wvt[...] = wv[...].T
    vq32[...] = dot(vx[...], wq[...]).astype(BF).astype(F32) * 0.125
    vkey[...] = dot(vx[...], wk[...]).astype(BF)
    vk32[...] = vkey[...].astype(F32)
    vval = dot(vx[...], wv[...]).astype(BF)
    vv32[...] = vval.astype(F32)

    member_row = mem[...]
    member = iota((VN, N), 0) == member_row
    k_own = dot(xall[pl.ds(0, N), :], wk[...]).astype(BF)
    v_own = dot(xall[pl.ds(0, N), :], wv[...]).astype(BF)
    lane = iota((VN, 128), 1)
    part_max = jnp.zeros((VN, 128), F32)
    part_sum = jnp.zeros((VN, 128), F32)
    odd = iota((VN, 128), 1) >= HD
    scored = []
    for w in range(H // 2):
        pair = slice(w * 128, w * 128 + 128)
        vqp = vq32[:, pair]
        vqp = jnp.concatenate([jnp.where(odd, 0.0, vqp), jnp.where(odd, vqp, 0.0)], axis=0)
        scored.append(dot(vqp.astype(BF), k_own[:, pair], NT))
    parts = []
    for w in range(H // 2):
        stack = []
        for i in range(2):
            s = jnp.where(member, scored[w][i * VN : (i + 1) * VN, :], NEG)
            top = jnp.max(s, axis=1, keepdims=True)
            p = jnp.where(member, jnp.exp(s - top), 0.0)
            part_max = jnp.where(lane == 2 * w + i, top, part_max)
            part_sum = jnp.where(lane == 2 * w + i, jnp.sum(p, axis=1, keepdims=True), part_sum)
            high = p.astype(BF)
            stack += [high, (p - high.astype(F32)).astype(BF)]
        parts.append(jnp.concatenate(stack, axis=0))
    for w in range(H // 2):
        pair = slice(w * 128, w * 128 + 128)
        o = dot(parts[w], v_own[:, pair])
        even, uneven = o[:VN] + o[VN : 2 * VN], o[2 * VN : 3 * VN] + o[3 * VN :]
        part[:, pair] = jnp.where(odd, uneven, even)
    part[:, pl.ds(D, 128)] = part_max
    part[:, pl.ds(D + 128, 128)] = part_sum
    pl.semaphore_wait(barrier, 127)
    for i in range(1, 8):
        pltpu.make_async_remote_copy(
            part.at[pl.ds(pl.multiple_of(others[i] * 8, 8), 8)], r1.at[g],
            s1s, s1r, device_id=(others[i], d), device_id_type=MESH,
        ).start()
    r1[g] = part[pl.ds(pl.multiple_of(g * 8, 8), 8), :]

    up, down = wrap(d + 1, 16), wrap(d + 15, 16)
    to_up = pltpu.make_async_remote_copy(
        xall.at[pl.ds(N - HALO, HALO)], xall.at[pl.ds(N + HALO, HALO)],
        halo_s.at[0], halo_r.at[0], device_id=(g, up), device_id_type=MESH,
    )
    to_down = pltpu.make_async_remote_copy(
        xall.at[pl.ds(0, HALO)], xall.at[pl.ds(N, HALO)],
        halo_s.at[1], halo_r.at[1], device_id=(g, down), device_id_type=MESH,
    )
    to_up.start()
    to_down.start()

    tx = [wrap(x + i, 4) * 2 for i in range(4)]
    tc = [c, 1 - c]
    ty = [wrap(y + i, 4) for i in range(4)]
    tz = [wrap(z + i, 4) * 4 for i in range(4)]

    def post(group):
        for kz in range(4):
            for ky in range(4):
                if group + kz + ky == 0:
                    continue
                tg = tx[(group // 2 + kz + ky) % 4] + tc[group % 2]
                td = tz[kz] + ty[ky]
                pltpu.make_async_remote_copy(
                    send.at[pl.ds(pl.multiple_of((tg * 16 + td) * CAP, CAP), CAP)],
                    xall.at[pl.ds(EXP0 + group * BLK + (kz * 4 + ky) * CAP, CAP)],
                    ssem, rsem.at[group], device_id=(tg, td), device_id_type=MESH,
                ).start()

    post(0)
    post(1)
    me = g * 16 + d
    xall[pl.ds(EXP0, CAP), :] = send[pl.ds(pl.multiple_of(me * CAP, CAP), CAP), :]

    win = nbr[...] - HALO
    win = jnp.where(win < 0, win + EXP0, win)
    win = jnp.where(iota((8, N), 0) < length[...], win, -1)
    for r in range(0, EXP0, 64):
        row = iota((64, N), 0) + r
        count = jnp.zeros((64, N), F32)
        for e in range(8):
            count = count + jnp.where(win[e : e + 1, :] == row, 1.0, 0.0)
        bias[pl.ds(r, 64), :] = jnp.where(count > 0.0, jnp.log(jnp.maximum(count, 1.0)), NEG)
    source = slot[...] // CAP
    sg, sd = source // 16, source % 16
    kz = (z - sd // 4 + 4) % 4
    ky = (y - sd % 4 + 4) % 4
    kc = (c - sg % 2 + 2) % 2
    kx = (x - sg // 2 + 4) % 4
    jx = (kx - kz - ky + 8) % 4
    spot = (jx * 2 + kc) * BLK + (kz * 4 + ky) * CAP + slot[...] % CAP

    def expander_bias(i, carry):
        r = pl.multiple_of(i * 64, 64)
        row = iota((64, N), 0) + r
        hit = spot[0:1, :] == row
        for e in range(1, 4):
            hit = hit | (spot[e : e + 1, :] == row)
        bias[pl.ds(EXP0 + r, 64), :] = jnp.where(hit, 0.0, NEG)
        return carry

    lax.fori_loop(0, GROUPS * BLK // 64, expander_bias, 0)

    vvt = vval.T
    vbias[...] = jnp.where(member, 0.0, NEG)
    add = vbias[...]
    scored = [dot(vkey[:, h // 2 * 128 : h // 2 * 128 + 128], qm[h], NT) for h in range(H)]
    weighed = []
    for h in range(H):
        s = scored[h] + add
        top = jnp.max(s, axis=0, keepdims=True)
        m_ref[h : h + 1, :] = top
        weighed.append(jnp.exp((s - top).astype(BF)))
    ones = jnp.ones((VR - HD, BLK), BF)
    for h in range(H):
        vals = jnp.concatenate([vvt[h * HD : (h + 1) * HD, :], ones[:, :VN]], axis=0)
        acc[h] = dot(vals, weighed[h])[:AR, :]
        vt[h, pl.ds(HD, VR - HD), :] = ones

    def wait_bytes(like, sem):
        pltpu.make_async_copy(like, like, sem).wait()

    expand = expander(128)

    def combine(parts):
        tops = [q[:, D : D + 128] for q in parts]
        top = functools.reduce(jnp.maximum, tops)
        scale = [jnp.exp(t - top) for t in tops]
        total = functools.reduce(jnp.add, [q[:, D + 128 :] * f for q, f in zip(parts, scale)])
        wide = dot(jnp.concatenate(scale, axis=0), expand, precision=lax.Precision.HIGHEST)
        n = parts[0].shape[0]
        mixed = functools.reduce(
            jnp.add, [q[:, :D] * wide[i * n : (i + 1) * n, :] for i, q in enumerate(parts)]
        )
        return mixed, top, total

    def block(b, carry):
        @pl.when(b == 0)
        def _():
            wait_bytes(r1.at[pl.ds(0, 7)], s1r)
            mixed, top, total = combine([r1[i] for i in range(8)])
            for i in range(8):
                c1[i, :, pl.ds(0, D)] = mixed[i : i + 1, :]
                c1[i, :, pl.ds(D, 128)] = top[i : i + 1, :]
                c1[i, :, pl.ds(D + 128, 128)] = total[i : i + 1, :]

            for i in range(8):
                @pl.when(d != i)
                def _():
                    pltpu.make_async_remote_copy(
                        c1.at[i], r2.at[d], s2s, s2r, device_id=(g, i), device_id_type=MESH
                    ).start()

            @pl.when(d < 8)
            def _():
                r2[d] = c1[d]

        @pl.when(b == 0)
        def _():
            post(2)
            post(3)

        @pl.when((b == OWN_BLOCKS) & (d < 8))
        def _():
            wait_bytes(r2.at[pl.ds(0, 15)], s2r)
            mixed, top, total = combine([r2[i] for i in range(16)])
            v = g * 8 + d
            vq, vk, vv = vq32[pl.ds(v, 1), :], vk32[pl.ds(v, 1), :], vv32[pl.ds(v, 1), :]
            eight = lambda row: jnp.broadcast_to(row, (8, row.shape[1]))
            own = dot(eight(vq * vk), expand, NT, precision=lax.Precision.HIGHEST)[0:1, :]
            peak = jnp.maximum(top, own)
            old, new = jnp.exp(top - peak), jnp.exp(own - peak)
            denom = total * old + new
            factors = jnp.concatenate([old, new, denom], axis=0)
            factors = jnp.concatenate([factors, jnp.zeros((5, 128), F32)], axis=0)
            wide = dot(factors, expand, precision=lax.Precision.HIGHEST)
            va = (mixed * wide[0:1, :] + wide[1:2, :] * vv) / wide[2:3, :]
            proj = dot(eight(va).astype(BF), wo[...])
            u = eight(vx_row(v)) + proj
            vrow[0] = norm(u, ga[...]).astype(BF).astype(F32)[0:1, :]
            for i in range(1, 16):
                pltpu.make_async_remote_copy(
                    vrow.at[0], r3a.at[d], s3s, s3r,
                    device_id=(g, wrap(d + i, 16)), device_id_type=MESH,
                ).start()
            r3a[d] = vrow[0]

        @pl.when(b == OWN_BLOCKS)
        def _():
            post(4)
            post(5)

        @pl.when(b == FIRST_EXP + 1)
        def _():
            @pl.when(d < 8)
            def _():
                wait_bytes(r3a.at[pl.ds(0, 7)], s3r)

            @pl.when(d >= 8)
            def _():
                wait_bytes(r3a.at[pl.ds(0, 8)], s3r)

            r3[g] = r3a[:, 0, :]
            for i in range(1, 8):
                pltpu.make_async_remote_copy(
                    r3.at[g], r3.at[g], s4s, s4r, device_id=(others[i], d), device_id_type=MESH
                ).start()

        @pl.when(b == FIRST_EXP + 1)
        def _():
            post(6)
            post(7)

        @pl.when(b == OWN_BLOCKS)
        def _():
            to_up.wait_recv()
            to_down.wait_recv()

        @pl.when(b == FIRST_EXP)
        def _():
            wait_bytes(xall.at[pl.ds(EXP0, 15 * CAP)], rsem.at[0])

        @pl.when(b > FIRST_EXP)
        def _():
            wait_bytes(xall.at[pl.ds(EXP0, 16 * CAP)], rsem.at[b - FIRST_EXP])

        r = pl.multiple_of(b * BLK, BLK)
        xb = xall[pl.ds(r, BLK), :]
        kblk[...] = dot(xb, wk[...]).astype(BF)
        vals = dot(wvt[...], xb, NT).astype(BF)
        for h in range(H):
            vt[h, pl.ds(0, HD), :] = vals[h * HD : (h + 1) * HD, :]
        add = bias[pl.ds(r, BLK), :]
        scored = [dot(kblk[:, h // 2 * 128 : h // 2 * 128 + 128], qm[h], NT) for h in range(H)]
        weighed = []
        for h in range(H):
            s = scored[h] + add
            old = m_ref[h : h + 1, :]
            top = jnp.maximum(old, jnp.max(s, axis=0, keepdims=True))
            m_ref[h : h + 1, :] = top
            weighed.append((jnp.exp((s - top).astype(BF)), jnp.exp(old - top)))
        for h in range(H):
            p, keep = weighed[h]
            acc[h] = acc[h] * keep + dot(vt[h], p)[:AR, :]
        return carry

    def vx_row(v):
        return vx32_row(vx, v)

    loads[12].wait()
    lax.fori_loop(0, BLOCKS, block, 0)

    wait_bytes(r3.at[pl.ds(0, 7)], s4r)
    vout[...] = r3[...].reshape(VN, D).astype(BF)
    last = pltpu.make_async_copy(vout, vout_hbm, out_sem.at[2])
    last.start()

    for h in range(H):
        span = slice(h * HD, (h + 1) * HD)
        att[span, :] = (acc[h, :HD, :] * (1.0 / acc[h, HD : HD + 1, :])).astype(BF)
    loads[13].wait()
    loads[14].wait()
    att[...] = att[...].T
    chunks = [pl.ds(r, BLK) for r in range(0, N, BLK)]
    settled = []
    for at in chunks:
        mixed = xall[at, :].astype(F32) + dot(att[at, :], wo[...])
        settled.append(norm(mixed, ga[...]).astype(BF))
    for i, at in enumerate(chunks):
        hidden = jnp.maximum(dot(settled[i], wu[...]), 0.0).astype(BF)
        total = settled[i].astype(F32) + dot(hidden, wd[...])
        outs[at, :] = norm(total, gf[...]).astype(BF)
        pltpu.make_async_copy(outs.at[at], out_hbm.at[at], out_sem.at[i]).start()

    to_up.wait_send()
    to_down.wait_send()
    wait_bytes(send.at[pl.ds(0, 127 * CAP)], ssem)
    wait_bytes(part.at[pl.ds(0, 56)], s1s)

    @pl.when(d < 8)
    def _():
        wait_bytes(c1.at[pl.ds(0, 7)], s2s)
        wait_bytes(r2.at[pl.ds(0, 15), :, pl.ds(0, D)], s3s)

    @pl.when(d >= 8)
    def _():
        wait_bytes(c1, s2s)

    wait_bytes(r3.at[pl.ds(0, 7)], s4s)
    for r in range(0, N, BLK):
        at = pl.ds(r, BLK)
        pltpu.make_async_copy(outs.at[at], out_hbm.at[at], out_sem.at[r // BLK]).wait()
    last.wait()


def vx32_row(vx, v):
    hot = (iota((8, VN), 1) == v).astype(F32).astype(BF)
    return dot(hot, vx[...])[0:1, :]


def hand_over(node, virtual, node_out, virtual_out, held, vheld, sem):
    steps = [(virtual, vheld, virtual_out)]
    for i in range(4):
        at = pl.ds(i * 128, 128)
        steps.append((node.at[at], held.at[at], node_out.at[at]))
    loads = [pltpu.make_async_copy(a, b, sem.at[0, i]) for i, (a, b, _) in enumerate(steps)]
    stores = [pltpu.make_async_copy(b, c, sem.at[1, i]) for i, (_, b, c) in enumerate(steps)]
    for load in loads:
        load.start()
    for load, store in zip(loads, stores):
        load.wait()
        store.start()
    for store in stores:
        store.wait()


def shards(
    node_input, virtual_input, w_query, w_key, w_value, w_out, w_up, w_down, gain_attn, gain_ffn,
    local_nbr, local_len, send_rows, exp_slot, membership,
):
    args = (
        node_input, virtual_input, w_query, w_key, w_value, w_out, w_up, w_down,
        gain_attn.reshape(1, D), gain_ffn.reshape(1, D), local_nbr.T, local_len.reshape(1, N),
        send_rows[0].T, exp_slot.T, membership.reshape(1, N),
    )
    vmem = pltpu.VMEM
    dma = pltpu.SemaphoreType.DMA
    scratch = [
        vmem((ROWS, D), BF), vmem((VN, D), BF), vmem((D, D), BF), vmem((D, D), BF),
        vmem((D, D), BF), vmem((D, D), BF), vmem((D, 4 * D), BF), vmem((4 * D, D), BF),
        vmem((1, D), F32), vmem((1, D), F32), vmem((8, N), jnp.int32), vmem((1, N), jnp.int32),
        vmem((CAP, 128), jnp.int32), vmem((4, N), jnp.int32), vmem((1, N), jnp.int32),
        vmem((128 * CAP, D), BF), vmem((D, D), BF), vmem((H, N, 128), BF), vmem((ROWS, N), F32),
        vmem((BLK, D), BF), vmem((H, VR, BLK), BF), vmem((H, N), F32),
        vmem((H, AR, N), F32), vmem((D, N), BF), vmem((N, D), BF),
        vmem((VN, D), F32), vmem((VN, D), F32), vmem((VN, D), F32), vmem((VN, D), BF),
        vmem((VN, N), F32), vmem((VN, PART), F32), vmem((8, 8, PART), F32),
        vmem((8, 1, PART), F32), vmem((16, 1, PART), F32), vmem((8, 1, D), F32),
        vmem((8, 8, D), F32), vmem((1, 1, D), F32), vmem((VN, D), BF),
        dma((15,)), dma((3,)), dma, dma((GROUPS,)), dma((2,)), dma((2,)),
        dma, dma, dma, dma, dma, dma, dma, dma,
    ]
    hbm = pl.BlockSpec(memory_space=pl.ANY)
    node, virtual = pl.pallas_call(
        kernel,
        out_shape=(
            jax.ShapeDtypeStruct((N, D), BF),
            jax.ShapeDtypeStruct((VN, D), BF),
        ),
        in_specs=[hbm] * len(args),
        out_specs=(hbm, hbm),
        scratch_shapes=scratch,
        compiler_params=pltpu.CompilerParams(
            collective_id=0, has_side_effects=True, vmem_limit_bytes=56 * 1024 * 1024
        ),
    )(*args)
    return pl.pallas_call(
        hand_over,
        out_shape=(
            jax.ShapeDtypeStruct((N, D), BF),
            jax.ShapeDtypeStruct((VN, D), BF),
        ),
        in_specs=[hbm] * 2,
        out_specs=(hbm, hbm),
        scratch_shapes=[vmem((N, D), BF), vmem((VN, D), BF), dma((2, 5))],
        compiler_params=pltpu.CompilerParams(vmem_limit_bytes=60 * 1024 * 1024),
    )(node, virtual)


def solution(mesh):
    rows = P(("group", "dom"), None)
    line = P(("group", "dom"))
    placed = (
        rows, P(), P(), P(), P(), P(), P(), P(), P(), P(),
        rows, line, P(("group", "dom"), None, None), rows, line,
    )
    return jax.shard_map(
        shards, mesh=mesh, in_specs=placed, out_specs=(rows, P()), check_vma=False
    )
```

```python
import functools

import jax
import jax.numpy as jnp
from jax import lax
from jax.experimental import pallas as pl
from jax.experimental.pallas import tpu as pltpu
from jax.sharding import PartitionSpec as P

MESH = pl.DeviceIdType.MESH
BF = jnp.bfloat16
F32 = jnp.float32
NEG = -1e30

D = 512
H = 8
HD = D // H
N = 512
VN = 64
HALO = 128
CAP = 16
BLK = 256
OWN_BLOCKS = N // BLK
FIRST_EXP = OWN_BLOCKS + 1
GROUPS = 8
BLOCKS = FIRST_EXP + GROUPS
ROWS = BLOCKS * BLK
EXP0 = FIRST_EXP * BLK
PART = D + 256
VR = HD + 16
AR = HD + 8
AHEAD = 6
FIRST = 2


def dot(a, b, dims=((1,), (0,)), precision=None):
    return lax.dot_general(a, b, (dims, ((), ())), precision=precision, preferred_element_type=F32)


NT = ((1,), (1,))


def iota(shape, dim):
    return lax.broadcasted_iota(jnp.int32, shape, dim)


def norm(u, gain):
    center = u - jnp.mean(u, axis=-1, keepdims=True)
    spread = jnp.mean(center * center, axis=-1, keepdims=True)
    return center * lax.rsqrt(spread + 1e-05) * gain


def expander(rows):
    return (iota((rows, D), 1) // HD == iota((rows, D), 0)).astype(F32)


def wrap(value, size):
    return jnp.where(value >= size, value - size, value)


def kernel(
    x_hbm, vx_hbm, wq_hbm, wk_hbm, wv_hbm, wo_hbm, wu_hbm, wd_hbm, ga_hbm, gf_hbm,
    nbr_hbm, len_hbm, rows_hbm, slot_hbm, mem_hbm,
    outs, vout,
    xall, vx, wq, wk, wv, wo, wu, wd, ga, gf, nbr, length, rows, slot, mem,
    send, wvt, qm, bias, kblk, vt, m_ref, acc, att,
    vq32, vk32, vv32, vkey, vbias, part, r1, c1, r2, r3a, r3, vrow,
    in_sem, ssem, rsem, halo_s, halo_r, s1s, s1r, s2s, s2r, s3s, s3r, s4s, s4r,
):
    g = lax.axis_index("group")
    d = lax.axis_index("dom")
    x, c = g // 2, g % 2
    z, y = d // 4, d % 4

    order = [
        (x_hbm, xall.at[pl.ds(0, N)]), (rows_hbm, rows), (wq_hbm, wq), (wk_hbm, wk), (wv_hbm, wv),
        (vx_hbm, vx), (mem_hbm, mem), (len_hbm, length), (nbr_hbm, nbr), (slot_hbm, slot),
        (ga_hbm, ga), (gf_hbm, gf), (wo_hbm, wo), (wu_hbm, wu), (wd_hbm, wd),
    ]
    loads = [pltpu.make_async_copy(a, b, in_sem.at[i]) for i, (a, b) in enumerate(order)]
    for load in loads:
        load.start()

    barrier = pltpu.get_barrier_semaphore()
    others = [wrap(g + i, H) for i in range(8)]

    def greet(dom, first):
        for i in range(first, 8):
            pl.semaphore_signal(barrier, inc=1, device_id=(others[i], dom), device_id_type=MESH)

    greet(d, 1)

    def greet_dom(i, carry):
        greet(wrap(d + i, 16), 0)
        return carry

    lax.fori_loop(1, 16, greet_dom, 0)

    loads[0].wait()
    loads[1].wait()
    picks = rows[...]
    lanes16 = iota((CAP, N), 1)
    for chunk in range(8):
        hot = jnp.concatenate(
            [
                (picks[:, chunk * 16 + i : chunk * 16 + i + 1] == lanes16).astype(F32).astype(BF)
                for i in range(16)
            ],
            axis=0,
        )
        send[pl.ds(chunk * 256, 256), :] = dot(hot, xall[pl.ds(0, N), :]).astype(BF)

    up, down = wrap(d + 1, 16), wrap(d + 15, 16)
    to_up = pltpu.make_async_remote_copy(
        xall.at[pl.ds(N - HALO, HALO)], xall.at[pl.ds(N + HALO, HALO)],
        halo_s.at[0], halo_r.at[0], device_id=(g, up), device_id_type=MESH,
    )
    to_down = pltpu.make_async_remote_copy(
        xall.at[pl.ds(0, HALO)], xall.at[pl.ds(N, HALO)],
        halo_s.at[1], halo_r.at[1], device_id=(g, down), device_id_type=MESH,
    )

    tx = [wrap(x + i, 4) * 2 for i in range(4)]
    tc = [c, 1 - c]
    ty = [wrap(y + i, 4) for i in range(4)]
    tz = [wrap(z + i, 4) * 4 for i in range(4)]

    def post(group):
        for kz in range(4):
            for ky in range(4):
                if group + kz + ky == 0:
                    continue
                tg = tx[(group // 2 + kz + ky) % 4] + tc[group % 2]
                td = tz[kz] + ty[ky]
                pltpu.make_async_remote_copy(
                    send.at[pl.ds(pl.multiple_of((tg * 16 + td) * CAP, CAP), CAP)],
                    xall.at[pl.ds(EXP0 + group * BLK + (kz * 4 + ky) * CAP, CAP)],
                    ssem, rsem.at[group], device_id=(tg, td), device_id_type=MESH,
                ).start()

    late = jnp.minimum(x, 2) + jnp.minimum(y, 2) + z >= 5

    def begin():
        to_up.start()
        to_down.start()
        for group in range(FIRST):
            post(group)

    @pl.when(late)
    def _():
        pl.semaphore_wait(barrier, 127)
        begin()

    for i in range(2, 12):
        loads[i].wait()
    half = iota((BLK, 128), 1) // HD
    for r in range(0, N, BLK):
        q = (dot(xall[pl.ds(r, BLK), :], wq[...]).astype(BF) * 0.125).astype(F32)
        for h in range(H):
            pair = q[:, h // 2 * 128 : h // 2 * 128 + 128]
            qm[h, pl.ds(r, BLK), :] = jnp.where(half == h % 2, pair, 0.0).astype(BF)
    wvt[...] = wv[...].T
    vq32[...] = dot(vx[...], wq[...]).astype(BF).astype(F32) * 0.125
    vkey[...] = dot(vx[...], wk[...]).astype(BF)
    vk32[...] = vkey[...].astype(F32)
    vval = dot(vx[...], wv[...]).astype(BF)
    vv32[...] = vval.astype(F32)

    member_row = mem[...]
    member = iota((VN, N), 0) == member_row
    k_own = dot(xall[pl.ds(0, N), :], wk[...]).astype(BF)
    v_own = dot(xall[pl.ds(0, N), :], wv[...]).astype(BF)
    lane = iota((VN, 128), 1)
    part_max = jnp.zeros((VN, 128), F32)
    part_sum = jnp.zeros((VN, 128), F32)
    odd = iota((VN, 128), 1) >= HD
    scored = []
    for w in range(H // 2):
        pair = slice(w * 128, w * 128 + 128)
        vqp = vq32[:, pair]
        vqp = jnp.concatenate([jnp.where(odd, 0.0, vqp), jnp.where(odd, vqp, 0.0)], axis=0)
        scored.append(dot(vqp.astype(BF), k_own[:, pair], NT))
    parts = []
    for w in range(H // 2):
        stack = []
        for i in range(2):
            s = jnp.where(member, scored[w][i * VN : (i + 1) * VN, :], NEG)
            top = jnp.max(s, axis=1, keepdims=True)
            p = jnp.where(member, jnp.exp(s - top), 0.0)
            part_max = jnp.where(lane == 2 * w + i, top, part_max)
            part_sum = jnp.where(lane == 2 * w + i, jnp.sum(p, axis=1, keepdims=True), part_sum)
            high = p.astype(BF)
            stack += [high, (p - high.astype(F32)).astype(BF)]
        parts.append(jnp.concatenate(stack, axis=0))
    for w in range(H // 2):
        pair = slice(w * 128, w * 128 + 128)
        o = dot(parts[w], v_own[:, pair])
        even, uneven = o[:VN] + o[VN : 2 * VN], o[2 * VN : 3 * VN] + o[3 * VN :]
        part[:, pair] = jnp.where(odd, uneven, even)
    part[:, pl.ds(D, 128)] = part_max
    part[:, pl.ds(D + 128, 128)] = part_sum

    @pl.when(jnp.logical_not(late))
    def _():
        pl.semaphore_wait(barrier, 127)

    for i in range(1, 8):
        pltpu.make_async_remote_copy(
            part.at[pl.ds(pl.multiple_of(others[i] * 8, 8), 8)], r1.at[g],
            s1s, s1r, device_id=(others[i], d), device_id_type=MESH,
        ).start()
    r1[g] = part[pl.ds(pl.multiple_of(g * 8, 8), 8), :]

    @pl.when(jnp.logical_not(late))
    def _():
        begin()

    for group in range(FIRST, AHEAD):
        post(group)
    me = g * 16 + d
    xall[pl.ds(EXP0, CAP), :] = send[pl.ds(pl.multiple_of(me * CAP, CAP), CAP), :]

    win = nbr[...] - HALO
    win = jnp.where(win < 0, win + EXP0, win)
    win = jnp.where(iota((8, N), 0) < length[...], win, -1)
    for r in range(0, EXP0, 64):
        row = iota((64, N), 0) + r
        count = jnp.zeros((64, N), F32)
        for e in range(8):
            count = count + jnp.where(win[e : e + 1, :] == row, 1.0, 0.0)
        bias[pl.ds(r, 64), :] = jnp.where(count > 0.0, jnp.log(jnp.maximum(count, 1.0)), NEG)
    source = slot[...] // CAP
    sg, sd = source // 16, source % 16
    kz = (z - sd // 4 + 4) % 4
    ky = (y - sd % 4 + 4) % 4
    kc = (c - sg % 2 + 2) % 2
    kx = (x - sg // 2 + 4) % 4
    jx = (kx - kz - ky + 8) % 4
    spot = (jx * 2 + kc) * BLK + (kz * 4 + ky) * CAP + slot[...] % CAP

    def expander_bias(i, carry):
        r = pl.multiple_of(i * 64, 64)
        row = iota((64, N), 0) + r
        hit = spot[0:1, :] == row
        for e in range(1, 4):
            hit = hit | (spot[e : e + 1, :] == row)
        bias[pl.ds(EXP0 + r, 64), :] = jnp.where(hit, 0.0, NEG)
        return carry

    lax.fori_loop(0, GROUPS * BLK // 64, expander_bias, 0)

    vvt = vval.T
    vbias[...] = jnp.where(member, 0.0, NEG)
    add = vbias[...]
    scored = [dot(vkey[:, h // 2 * 128 : h // 2 * 128 + 128], qm[h], NT) for h in range(H)]
    weighed = []
    for h in range(H):
        s = scored[h] + add
        top = jnp.max(s, axis=0, keepdims=True)
        m_ref[h : h + 1, :] = top
        weighed.append(jnp.exp((s - top).astype(BF)))
    ones = jnp.ones((VR - HD, BLK), BF)
    for h in range(H):
        vals = jnp.concatenate([vvt[h * HD : (h + 1) * HD, :], ones[:, :VN]], axis=0)
        acc[h] = dot(vals, weighed[h])[:AR, :]
        vt[h, pl.ds(HD, VR - HD), :] = ones

    def wait_bytes(like, sem):
        pltpu.make_async_copy(like, like, sem).wait()

    expand = expander(128)

    def combine(parts):
        tops = [q[:, D : D + 128] for q in parts]
        top = functools.reduce(jnp.maximum, tops)
        scale = [jnp.exp(t - top) for t in tops]
        total = functools.reduce(jnp.add, [q[:, D + 128 :] * f for q, f in zip(parts, scale)])
        wide = dot(jnp.concatenate(scale, axis=0), expand, precision=lax.Precision.HIGHEST)
        n = parts[0].shape[0]
        mixed = functools.reduce(
            jnp.add, [q[:, :D] * wide[i * n : (i + 1) * n, :] for i, q in enumerate(parts)]
        )
        return mixed, top, total

    def block(b, carry):
        @pl.when(b == 0)
        def _():
            wait_bytes(r1.at[pl.ds(0, 7)], s1r)
            mixed, top, total = combine([r1[i] for i in range(8)])
            for i in range(8):
                c1[i, :, pl.ds(0, D)] = mixed[i : i + 1, :]
                c1[i, :, pl.ds(D, 128)] = top[i : i + 1, :]
                c1[i, :, pl.ds(D + 128, 128)] = total[i : i + 1, :]

            for i in range(8):
                @pl.when(d != i + 8)
                def _():
                    pltpu.make_async_remote_copy(
                        c1.at[i], r2.at[d], s2s, s2r, device_id=(g, i + 8), device_id_type=MESH
                    ).start()

            @pl.when(d >= 8)
            def _():
                r2[d] = c1[d - 8]

        @pl.when((b == FIRST_EXP + 6) & (d >= 8))
        def _():
            wait_bytes(r2.at[pl.ds(0, 15)], s2r)
            mixed, top, total = combine([r2[i] for i in range(16)])
            v = g * 8 + d - 8
            vq, vk, vv = vq32[pl.ds(v, 1), :], vk32[pl.ds(v, 1), :], vv32[pl.ds(v, 1), :]
            eight = lambda row: jnp.broadcast_to(row, (8, row.shape[1]))
            own = dot(eight(vq * vk), expand, NT, precision=lax.Precision.HIGHEST)[0:1, :]
            peak = jnp.maximum(top, own)
            old, new = jnp.exp(top - peak), jnp.exp(own - peak)
            denom = total * old + new
            factors = jnp.concatenate([old, new, denom], axis=0)
            factors = jnp.concatenate([factors, jnp.zeros((5, 128), F32)], axis=0)
            wide = dot(factors, expand, precision=lax.Precision.HIGHEST)
            va = (mixed * wide[0:1, :] + wide[1:2, :] * vv) / wide[2:3, :]
            proj = dot(eight(va).astype(BF), wo[...])
            u = eight(vx_row(v)) + proj
            vrow[0] = norm(u, ga[...]).astype(BF).astype(F32)[0:1, :]
            for i in range(1, 16):
                pltpu.make_async_remote_copy(
                    vrow.at[0], r3a.at[d - 8], s3s, s3r,
                    device_id=(g, wrap(d + i, 16)), device_id_type=MESH,
                ).start()
            r3a[d - 8] = vrow[0]

        @pl.when(b == OWN_BLOCKS)
        def _():
            to_up.wait_recv()
            to_down.wait_recv()

        @pl.when(b == FIRST_EXP)
        def _():
            wait_bytes(xall.at[pl.ds(EXP0, 15 * CAP)], rsem.at[0])

        @pl.when(b > FIRST_EXP)
        def _():
            wait_bytes(xall.at[pl.ds(EXP0, 16 * CAP)], rsem.at[b - FIRST_EXP])

        @pl.when(b == FIRST_EXP + 0)
        def _():
            post(AHEAD + 0)

        @pl.when(b == FIRST_EXP + 1)
        def _():
            post(AHEAD + 1)

        r = pl.multiple_of(b * BLK, BLK)
        xb = xall[pl.ds(r, BLK), :]
        kblk[...] = dot(xb, wk[...]).astype(BF)
        vals = dot(wvt[...], xb, NT).astype(BF)
        for h in range(H):
            vt[h, pl.ds(0, HD), :] = vals[h * HD : (h + 1) * HD, :]
        add = bias[pl.ds(r, BLK), :]
        scored = [dot(kblk[:, h // 2 * 128 : h // 2 * 128 + 128], qm[h], NT) for h in range(H)]
        weighed = []
        for h in range(H):
            s = scored[h] + add
            old = m_ref[h : h + 1, :]
            top = jnp.maximum(old, jnp.max(s, axis=0, keepdims=True))
            m_ref[h : h + 1, :] = top
            weighed.append((jnp.exp((s - top).astype(BF)), jnp.exp(old - top)))
        for h in range(H):
            p, keep = weighed[h]
            acc[h] = acc[h] * keep + dot(vt[h], p)[:AR, :]
        return carry

    def vx_row(v):
        return vx32_row(vx, v)

    loads[12].wait()
    lax.fori_loop(0, BLOCKS, block, 0)

    @pl.when(d < 8)
    def _():
        wait_bytes(r3a, s3r)

    @pl.when(d >= 8)
    def _():
        wait_bytes(r3a.at[pl.ds(0, 7)], s3r)

    r3[g] = r3a[:, 0, :]
    for i in range(1, 8):
        pltpu.make_async_remote_copy(
            r3.at[g], r3.at[g], s4s, s4r, device_id=(others[i], d), device_id_type=MESH
        ).start()

    for h in range(H):
        span = slice(h * HD, (h + 1) * HD)
        att[span, :] = (acc[h, :HD, :] * (1.0 / acc[h, HD : HD + 1, :])).astype(BF)
    loads[13].wait()
    loads[14].wait()
    att[...] = att[...].T
    chunks = [pl.ds(r, BLK) for r in range(0, N, BLK)]
    settled = []
    for at in chunks:
        mixed = xall[at, :].astype(F32) + dot(att[at, :], wo[...])
        settled.append(norm(mixed, ga[...]).astype(BF))
    for i, at in enumerate(chunks):
        hidden = jnp.maximum(dot(settled[i], wu[...]), 0.0).astype(BF)
        total = settled[i].astype(F32) + dot(hidden, wd[...])
        outs[at, :] = norm(total, gf[...]).astype(BF)

    wait_bytes(r3.at[pl.ds(0, 7)], s4r)
    vout[...] = r3[...].reshape(VN, D).astype(BF)

    to_up.wait_send()
    to_down.wait_send()
    wait_bytes(send.at[pl.ds(0, 127 * CAP)], ssem)
    wait_bytes(part.at[pl.ds(0, 56)], s1s)

    @pl.when(d < 8)
    def _():
        wait_bytes(c1, s2s)

    @pl.when(d >= 8)
    def _():
        wait_bytes(c1.at[pl.ds(0, 7)], s2s)
        wait_bytes(r2.at[pl.ds(0, 15), :, pl.ds(0, D)], s3s)

    wait_bytes(r3.at[pl.ds(0, 7)], s4s)


def vx32_row(vx, v):
    hot = (iota((8, VN), 1) == v).astype(F32).astype(BF)
    return dot(hot, vx[...])[0:1, :]


def hand_over(node, virtual, node_out, virtual_out, sem):
    copies = [pltpu.make_async_copy(virtual, virtual_out, sem.at[4])]
    for i in range(4):
        at = pl.ds(i * 128, 128)
        copies.append(pltpu.make_async_copy(node.at[at], node_out.at[at], sem.at[i]))
    for copy in copies:
        copy.start()
    for copy in copies:
        copy.wait()


def shards(
    node_input, virtual_input, w_query, w_key, w_value, w_out, w_up, w_down, gain_attn, gain_ffn,
    local_nbr, local_len, send_rows, exp_slot, membership,
):
    args = (
        node_input, virtual_input, w_query, w_key, w_value, w_out, w_up, w_down,
        gain_attn.reshape(1, D), gain_ffn.reshape(1, D), local_nbr.T, local_len.reshape(1, N),
        send_rows[0].T, exp_slot.T, membership.reshape(1, N),
    )
    vmem = pltpu.VMEM
    dma = pltpu.SemaphoreType.DMA
    scratch = [
        vmem((ROWS, D), BF), vmem((VN, D), BF), vmem((D, D), BF), vmem((D, D), BF),
        vmem((D, D), BF), vmem((D, D), BF), vmem((D, 4 * D), BF), vmem((4 * D, D), BF),
        vmem((1, D), F32), vmem((1, D), F32), vmem((8, N), jnp.int32), vmem((1, N), jnp.int32),
        vmem((CAP, 128), jnp.int32), vmem((4, N), jnp.int32), vmem((1, N), jnp.int32),
        vmem((128 * CAP, D), BF), vmem((D, D), BF), vmem((H, N, 128), BF), vmem((ROWS, N), F32),
        vmem((BLK, D), BF), vmem((H, VR, BLK), BF), vmem((H, N), F32),
        vmem((H, AR, N), F32), vmem((D, N), BF),
        vmem((VN, D), F32), vmem((VN, D), F32), vmem((VN, D), F32), vmem((VN, D), BF),
        vmem((VN, N), F32), vmem((VN, PART), F32), vmem((8, 8, PART), F32),
        vmem((8, 1, PART), F32), vmem((16, 1, PART), F32), vmem((8, 1, D), F32),
        vmem((8, 8, D), F32), vmem((1, 1, D), F32),
        dma((15,)), dma, dma((GROUPS,)), dma((2,)), dma((2,)),
        dma, dma, dma, dma, dma, dma, dma, dma,
    ]
    hbm = pl.BlockSpec(memory_space=pl.ANY)
    node, virtual = pl.pallas_call(
        kernel,
        out_shape=(vmem((N, D), BF), vmem((VN, D), BF)),
        in_specs=[hbm] * len(args),
        out_specs=(pl.BlockSpec(memory_space=vmem),) * 2,
        scratch_shapes=scratch,
        compiler_params=pltpu.CompilerParams(
            collective_id=0, has_side_effects=True, vmem_limit_bytes=56 * 1024 * 1024
        ),
    )(*args)
    return pl.pallas_call(
        hand_over,
        out_shape=(
            jax.ShapeDtypeStruct((N, D), BF),
            jax.ShapeDtypeStruct((VN, D), BF),
        ),
        in_specs=[pl.BlockSpec(memory_space=vmem)] * 2,
        out_specs=(hbm, hbm),
        scratch_shapes=[dma((5,))],
        compiler_params=pltpu.CompilerParams(vmem_limit_bytes=16 * 1024 * 1024),
    )(node, virtual)


def solution(mesh):
    rows = P(("group", "dom"), None)
    line = P(("group", "dom"))
    placed = (
        rows, P(), P(), P(), P(), P(), P(), P(), P(), P(),
        rows, line, P(("group", "dom"), None, None), rows, line,
    )
    return jax.shard_map(
        shards, mesh=mesh, in_specs=placed, out_specs=(rows, P()), check_vma=False
    )
```

```python
import functools

import jax
import jax.numpy as jnp
from jax import lax
from jax.experimental import pallas as pl
from jax.experimental.pallas import tpu as pltpu
from jax.sharding import PartitionSpec as P

MESH = pl.DeviceIdType.MESH
BF = jnp.bfloat16
F32 = jnp.float32
NEG = -1e30

D = 512
H = 8
HD = D // H
N = 512
VN = 64
HALO = 128
CAP = 16
BLK = 256
OWN_BLOCKS = N // BLK
FIRST_EXP = OWN_BLOCKS + 1
GROUPS = 8
BLOCKS = FIRST_EXP + GROUPS
ROWS = BLOCKS * BLK
EXP0 = FIRST_EXP * BLK
PART = D + 256
VR = HD + 16
AR = HD + 8
AHEAD = 6
FIRST = 2


def dot(a, b, dims=((1,), (0,)), precision=None):
    return lax.dot_general(a, b, (dims, ((), ())), precision=precision, preferred_element_type=F32)


NT = ((1,), (1,))


def iota(shape, dim):
    return lax.broadcasted_iota(jnp.int32, shape, dim)


def norm(u, gain):
    center = u - jnp.mean(u, axis=-1, keepdims=True)
    spread = jnp.mean(center * center, axis=-1, keepdims=True)
    return center * lax.rsqrt(spread + 1e-05) * gain


def expander(rows):
    return (iota((rows, D), 1) // HD == iota((rows, D), 0)).astype(F32)


def wrap(value, size):
    return jnp.where(value >= size, value - size, value)


def kernel(
    x_hbm, vx_hbm, wq_hbm, wk_hbm, wv_hbm, wo_hbm, wu_hbm, wd_hbm, ga_hbm, gf_hbm,
    nbr_hbm, len_hbm, rows_hbm, slot_hbm, mem_hbm,
    outs, vout,
    xall, vx, wq, wk, wv, wo, wu, wd, ga, gf, nbr, length, rows, slot, mem,
    send, wvt, qm, bias, kblk, vt, m_ref, acc, att,
    vq32, vk32, vv32, vkey, vbias, part, r1, c1, r2, r3a, r3, vrow,
    in_sem, ssem, rsem, halo_s, halo_r, s1s, s1r, s2s, s2r, s3s, s3r, s4s, s4r,
):
    g = lax.axis_index("group")
    d = lax.axis_index("dom")
    x, c = g // 2, g % 2
    z, y = d // 4, d % 4

    order = [
        (x_hbm, xall.at[pl.ds(0, N)]), (rows_hbm, rows), (wq_hbm, wq), (wk_hbm, wk), (wv_hbm, wv),
        (vx_hbm, vx), (mem_hbm, mem), (len_hbm, length), (nbr_hbm, nbr), (slot_hbm, slot),
        (ga_hbm, ga), (gf_hbm, gf), (wo_hbm, wo), (wu_hbm, wu), (wd_hbm, wd),
    ]
    loads = [pltpu.make_async_copy(a, b, in_sem.at[i]) for i, (a, b) in enumerate(order)]
    for load in loads[:2]:
        load.start()

    barrier = pltpu.get_barrier_semaphore()
    others = [wrap(g + i, H) for i in range(8)]

    def greet(dom, first):
        for i in range(first, 8):
            pl.semaphore_signal(barrier, inc=1, device_id=(others[i], dom), device_id_type=MESH)

    greet(d, 1)

    def greet_dom(i, carry):
        greet(wrap(d + i, 16), 0)
        return carry

    lax.fori_loop(1, 16, greet_dom, 0)

    for load in loads[2:]:
        load.start()

    loads[0].wait()
    loads[1].wait()
    picks = rows[...]
    lanes16 = iota((CAP, N), 1)
    for chunk in range(8):
        hot = jnp.concatenate(
            [
                (picks[:, chunk * 16 + i : chunk * 16 + i + 1] == lanes16).astype(F32).astype(BF)
                for i in range(16)
            ],
            axis=0,
        )
        send[pl.ds(chunk * 256, 256), :] = dot(hot, xall[pl.ds(0, N), :]).astype(BF)

    up, down = wrap(d + 1, 16), wrap(d + 15, 16)
    to_up = pltpu.make_async_remote_copy(
        xall.at[pl.ds(N - HALO, HALO)], xall.at[pl.ds(N + HALO, HALO)],
        halo_s.at[0], halo_r.at[0], device_id=(g, up), device_id_type=MESH,
    )
    to_down = pltpu.make_async_remote_copy(
        xall.at[pl.ds(0, HALO)], xall.at[pl.ds(N, HALO)],
        halo_s.at[1], halo_r.at[1], device_id=(g, down), device_id_type=MESH,
    )

    tx = [wrap(x + i, 4) * 2 for i in range(4)]
    tc = [c, 1 - c]
    ty = [wrap(y + i, 4) for i in range(4)]
    tz = [wrap(z + i, 4) * 4 for i in range(4)]

    def post(group):
        for kz in range(4):
            for ky in range(4):
                if group + kz + ky == 0:
                    continue
                tg = tx[(group // 2 + kz + ky) % 4] + tc[group % 2]
                td = tz[kz] + ty[ky]
                pltpu.make_async_remote_copy(
                    send.at[pl.ds(pl.multiple_of((tg * 16 + td) * CAP, CAP), CAP)],
                    xall.at[pl.ds(EXP0 + group * BLK + (kz * 4 + ky) * CAP, CAP)],
                    ssem, rsem.at[group], device_id=(tg, td), device_id_type=MESH,
                ).start()

    late = jnp.minimum(x, 2) + jnp.minimum(y, 2) + z >= 6

    def begin():
        to_up.start()
        to_down.start()
        for group in range(FIRST):
            post(group)

    @pl.when(late)
    def _():
        pl.semaphore_wait(barrier, 127)
        begin()

    for i in range(2, 12):
        loads[i].wait()
    half = iota((BLK, 128), 1) // HD
    for r in range(0, N, BLK):
        q = (dot(xall[pl.ds(r, BLK), :], wq[...]).astype(BF) * 0.125).astype(F32)
        for h in range(H):
            pair = q[:, h // 2 * 128 : h // 2 * 128 + 128]
            qm[h, pl.ds(r, BLK), :] = jnp.where(half == h % 2, pair, 0.0).astype(BF)
    wvt[...] = wv[...].T
    vq32[...] = dot(vx[...], wq[...]).astype(BF).astype(F32) * 0.125
    vkey[...] = dot(vx[...], wk[...]).astype(BF)
    vk32[...] = vkey[...].astype(F32)
    vval = dot(vx[...], wv[...]).astype(BF)
    vv32[...] = vval.astype(F32)

    member_row = mem[...]
    member = iota((VN, N), 0) == member_row
    k_own = dot(xall[pl.ds(0, N), :], wk[...]).astype(BF)
    v_own = dot(xall[pl.ds(0, N), :], wv[...]).astype(BF)
    lane = iota((VN, 128), 1)
    part_max = jnp.zeros((VN, 128), F32)
    part_sum = jnp.zeros((VN, 128), F32)
    odd = iota((VN, 128), 1) >= HD
    scored = []
    for w in range(H // 2):
        pair = slice(w * 128, w * 128 + 128)
        vqp = vq32[:, pair]
        vqp = jnp.concatenate([jnp.where(odd, 0.0, vqp), jnp.where(odd, vqp, 0.0)], axis=0)
        scored.append(dot(vqp.astype(BF), k_own[:, pair], NT))
    parts = []
    for w in range(H // 2):
        stack = []
        for i in range(2):
            s = jnp.where(member, scored[w][i * VN : (i + 1) * VN, :], NEG)
            top = jnp.max(s, axis=1, keepdims=True)
            p = jnp.where(member, jnp.exp(s - top), 0.0)
            part_max = jnp.where(lane == 2 * w + i, top, part_max)
            part_sum = jnp.where(lane == 2 * w + i, jnp.sum(p, axis=1, keepdims=True), part_sum)
            high = p.astype(BF)
            stack += [high, (p - high.astype(F32)).astype(BF)]
        parts.append(jnp.concatenate(stack, axis=0))
    for w in range(H // 2):
        pair = slice(w * 128, w * 128 + 128)
        o = dot(parts[w], v_own[:, pair])
        even, uneven = o[:VN] + o[VN : 2 * VN], o[2 * VN : 3 * VN] + o[3 * VN :]
        part[:, pair] = jnp.where(odd, uneven, even)
    part[:, pl.ds(D, 128)] = part_max
    part[:, pl.ds(D + 128, 128)] = part_sum

    @pl.when(jnp.logical_not(late))
    def _():
        pl.semaphore_wait(barrier, 127)

    for i in range(1, 8):
        pltpu.make_async_remote_copy(
            part.at[pl.ds(pl.multiple_of(others[i] * 8, 8), 8)], r1.at[g],
            s1s, s1r, device_id=(others[i], d), device_id_type=MESH,
        ).start()
    r1[g] = part[pl.ds(pl.multiple_of(g * 8, 8), 8), :]

    @pl.when(jnp.logical_not(late))
    def _():
        begin()

    for group in range(FIRST, AHEAD):
        post(group)
    me = g * 16 + d
    xall[pl.ds(EXP0, CAP), :] = send[pl.ds(pl.multiple_of(me * CAP, CAP), CAP), :]

    win = nbr[...] - HALO
    win = jnp.where(win < 0, win + EXP0, win)
    win = jnp.where(iota((8, N), 0) < length[...], win, -1)
    for r in range(0, EXP0, 64):
        row = iota((64, N), 0) + r
        count = jnp.zeros((64, N), F32)
        for e in range(8):
            count = count + jnp.where(win[e : e + 1, :] == row, 1.0, 0.0)
        bias[pl.ds(r, 64), :] = jnp.where(count > 0.0, jnp.log(jnp.maximum(count, 1.0)), NEG)
    source = slot[...] // CAP
    sg, sd = source // 16, source % 16
    kz = (z - sd // 4 + 4) % 4
    ky = (y - sd % 4 + 4) % 4
    kc = (c - sg % 2 + 2) % 2
    kx = (x - sg // 2 + 4) % 4
    jx = (kx - kz - ky + 8) % 4
    spot = (jx * 2 + kc) * BLK + (kz * 4 + ky) * CAP + slot[...] % CAP

    def expander_bias(i, carry):
        r = pl.multiple_of(i * 64, 64)
        row = iota((64, N), 0) + r
        hit = spot[0:1, :] == row
        for e in range(1, 4):
            hit = hit | (spot[e : e + 1, :] == row)
        bias[pl.ds(EXP0 + r, 64), :] = jnp.where(hit, 0.0, NEG)
        return carry

    lax.fori_loop(0, GROUPS * BLK // 64, expander_bias, 0)

    vvt = vval.T
    vbias[...] = jnp.where(member, 0.0, NEG)
    add = vbias[...]
    scored = [dot(vkey[:, h // 2 * 128 : h // 2 * 128 + 128], qm[h], NT) for h in range(H)]
    weighed = []
    for h in range(H):
        s = scored[h] + add
        top = jnp.max(s, axis=0, keepdims=True)
        m_ref[h : h + 1, :] = top
        weighed.append(jnp.exp((s - top).astype(BF)))
    ones = jnp.ones((VR - HD, BLK), BF)
    for h in range(H):
        vals = jnp.concatenate([vvt[h * HD : (h + 1) * HD, :], ones[:, :VN]], axis=0)
        acc[h] = dot(vals, weighed[h])[:AR, :]
        vt[h, pl.ds(HD, VR - HD), :] = ones

    def wait_bytes(like, sem):
        pltpu.make_async_copy(like, like, sem).wait()

    expand = expander(128)

    def combine(parts):
        tops = [q[:, D : D + 128] for q in parts]
        top = functools.reduce(jnp.maximum, tops)
        scale = [jnp.exp(t - top) for t in tops]
        total = functools.reduce(jnp.add, [q[:, D + 128 :] * f for q, f in zip(parts, scale)])
        wide = dot(jnp.concatenate(scale, axis=0), expand, precision=lax.Precision.HIGHEST)
        n = parts[0].shape[0]
        mixed = functools.reduce(
            jnp.add, [q[:, :D] * wide[i * n : (i + 1) * n, :] for i, q in enumerate(parts)]
        )
        return mixed, top, total

    def block(b, carry):
        @pl.when(b == 0)
        def _():
            wait_bytes(r1.at[pl.ds(0, 7)], s1r)
            mixed, top, total = combine([r1[i] for i in range(8)])
            for i in range(8):
                c1[i, :, pl.ds(0, D)] = mixed[i : i + 1, :]
                c1[i, :, pl.ds(D, 128)] = top[i : i + 1, :]
                c1[i, :, pl.ds(D + 128, 128)] = total[i : i + 1, :]

            for i in range(8):
                @pl.when(d != i + 8)
                def _():
                    pltpu.make_async_remote_copy(
                        c1.at[i], r2.at[d], s2s, s2r, device_id=(g, i + 8), device_id_type=MESH
                    ).start()

            @pl.when(d >= 8)
            def _():
                r2[d] = c1[d - 8]

        @pl.when((b == FIRST_EXP + 5) & (d >= 8))
        def _():
            wait_bytes(r2.at[pl.ds(0, 15)], s2r)
            mixed, top, total = combine([r2[i] for i in range(16)])
            v = g * 8 + d - 8
            vq, vk, vv = vq32[pl.ds(v, 1), :], vk32[pl.ds(v, 1), :], vv32[pl.ds(v, 1), :]
            eight = lambda row: jnp.broadcast_to(row, (8, row.shape[1]))
            own = dot(eight(vq * vk), expand, NT, precision=lax.Precision.HIGHEST)[0:1, :]
            peak = jnp.maximum(top, own)
            old, new = jnp.exp(top - peak), jnp.exp(own - peak)
            denom = total * old + new
            factors = jnp.concatenate([old, new, denom], axis=0)
            factors = jnp.concatenate([factors, jnp.zeros((5, 128), F32)], axis=0)
            wide = dot(factors, expand, precision=lax.Precision.HIGHEST)
            va = (mixed * wide[0:1, :] + wide[1:2, :] * vv) / wide[2:3, :]
            proj = dot(eight(va).astype(BF), wo[...])
            u = eight(vx_row(v)) + proj
            vrow[0] = norm(u, ga[...]).astype(BF).astype(F32)[0:1, :]
            for i in range(1, 16):
                pltpu.make_async_remote_copy(
                    vrow.at[0], r3a.at[d - 8], s3s, s3r,
                    device_id=(g, wrap(d + i, 16)), device_id_type=MESH,
                ).start()
            r3a[d - 8] = vrow[0]

        @pl.when(b == OWN_BLOCKS)
        def _():
            to_up.wait_recv()
            to_down.wait_recv()

        @pl.when(b == FIRST_EXP)
        def _():
            wait_bytes(xall.at[pl.ds(EXP0, 15 * CAP)], rsem.at[0])

        @pl.when(b > FIRST_EXP)
        def _():
            wait_bytes(xall.at[pl.ds(EXP0, 16 * CAP)], rsem.at[b - FIRST_EXP])

        @pl.when(b == FIRST_EXP + 0)
        def _():
            post(AHEAD + 0)

        @pl.when(b == FIRST_EXP + 1)
        def _():
            post(AHEAD + 1)

        r = pl.multiple_of(b * BLK, BLK)
        xb = xall[pl.ds(r, BLK), :]
        kblk[...] = dot(xb, wk[...]).astype(BF)
        vals = dot(wvt[...], xb, NT).astype(BF)
        for h in range(H):
            vt[h, pl.ds(0, HD), :] = vals[h * HD : (h + 1) * HD, :]
        add = bias[pl.ds(r, BLK), :]
        scored = [dot(kblk[:, h // 2 * 128 : h // 2 * 128 + 128], qm[h], NT) for h in range(H)]
        weighed = []
        for h in range(H):
            s = scored[h] + add
            old = m_ref[h : h + 1, :]
            top = jnp.maximum(old, jnp.max(s, axis=0, keepdims=True))
            m_ref[h : h + 1, :] = top
            weighed.append((jnp.exp((s - top).astype(BF)), jnp.exp(old - top)))
        for h in range(H):
            p, keep = weighed[h]
            acc[h] = acc[h] * keep + dot(vt[h], p)[:AR, :]
        return carry

    def vx_row(v):
        return vx32_row(vx, v)

    loads[12].wait()
    lax.fori_loop(0, BLOCKS, block, 0)

    @pl.when(d < 8)
    def _():
        wait_bytes(r3a, s3r)

    @pl.when(d >= 8)
    def _():
        wait_bytes(r3a.at[pl.ds(0, 7)], s3r)

    r3[g] = r3a[:, 0, :]
    for i in range(1, 8):
        pltpu.make_async_remote_copy(
            r3.at[g], r3.at[g], s4s, s4r, device_id=(others[i], d), device_id_type=MESH
        ).start()

    for h in range(H):
        span = slice(h * HD, (h + 1) * HD)
        att[span, :] = (acc[h, :HD, :] * (1.0 / acc[h, HD : HD + 1, :])).astype(BF)
    loads[13].wait()
    loads[14].wait()
    att[...] = att[...].T
    chunks = [pl.ds(r, BLK) for r in range(0, N, BLK)]
    settled = []
    for at in chunks:
        mixed = xall[at, :].astype(F32) + dot(att[at, :], wo[...])
        settled.append(norm(mixed, ga[...]).astype(BF))
    for i, at in enumerate(chunks):
        hidden = jnp.maximum(dot(settled[i], wu[...]), 0.0).astype(BF)
        total = settled[i].astype(F32) + dot(hidden, wd[...])
        outs[at, :] = norm(total, gf[...]).astype(BF)

    wait_bytes(r3.at[pl.ds(0, 7)], s4r)
    vout[...] = r3[...].reshape(VN, D).astype(BF)

    to_up.wait_send()
    to_down.wait_send()
    wait_bytes(send.at[pl.ds(0, 127 * CAP)], ssem)
    wait_bytes(part.at[pl.ds(0, 56)], s1s)

    @pl.when(d < 8)
    def _():
        wait_bytes(c1, s2s)

    @pl.when(d >= 8)
    def _():
        wait_bytes(c1.at[pl.ds(0, 7)], s2s)
        wait_bytes(r2.at[pl.ds(0, 15), :, pl.ds(0, D)], s3s)

    wait_bytes(r3.at[pl.ds(0, 7)], s4s)


def vx32_row(vx, v):
    hot = (iota((8, VN), 1) == v).astype(F32).astype(BF)
    return dot(hot, vx[...])[0:1, :]


def hand_over(node, virtual, node_out, virtual_out, sem):
    copies = [pltpu.make_async_copy(virtual, virtual_out, sem.at[4])]
    for i in range(4):
        at = pl.ds(i * 128, 128)
        copies.append(pltpu.make_async_copy(node.at[at], node_out.at[at], sem.at[i]))
    for copy in copies:
        copy.start()
    for copy in copies:
        copy.wait()


def shards(
    node_input, virtual_input, w_query, w_key, w_value, w_out, w_up, w_down, gain_attn, gain_ffn,
    local_nbr, local_len, send_rows, exp_slot, membership,
):
    args = (
        node_input, virtual_input, w_query, w_key, w_value, w_out, w_up, w_down,
        gain_attn.reshape(1, D), gain_ffn.reshape(1, D), local_nbr.T, local_len.reshape(1, N),
        send_rows[0].T, exp_slot.T, membership.reshape(1, N),
    )
    vmem = pltpu.VMEM
    dma = pltpu.SemaphoreType.DMA
    scratch = [
        vmem((ROWS, D), BF), vmem((VN, D), BF), vmem((D, D), BF), vmem((D, D), BF),
        vmem((D, D), BF), vmem((D, D), BF), vmem((D, 4 * D), BF), vmem((4 * D, D), BF),
        vmem((1, D), F32), vmem((1, D), F32), vmem((8, N), jnp.int32), vmem((1, N), jnp.int32),
        vmem((CAP, 128), jnp.int32), vmem((4, N), jnp.int32), vmem((1, N), jnp.int32),
        vmem((128 * CAP, D), BF), vmem((D, D), BF), vmem((H, N, 128), BF), vmem((ROWS, N), F32),
        vmem((BLK, D), BF), vmem((H, VR, BLK), BF), vmem((H, N), F32),
        vmem((H, AR, N), F32), vmem((D, N), BF),
        vmem((VN, D), F32), vmem((VN, D), F32), vmem((VN, D), F32), vmem((VN, D), BF),
        vmem((VN, N), F32), vmem((VN, PART), F32), vmem((8, 8, PART), F32),
        vmem((8, 1, PART), F32), vmem((16, 1, PART), F32), vmem((8, 1, D), F32),
        vmem((8, 8, D), F32), vmem((1, 1, D), F32),
        dma((15,)), dma, dma((GROUPS,)), dma((2,)), dma((2,)),
        dma, dma, dma, dma, dma, dma, dma, dma,
    ]
    hbm = pl.BlockSpec(memory_space=pl.ANY)
    node, virtual = pl.pallas_call(
        kernel,
        out_shape=(vmem((N, D), BF), vmem((VN, D), BF)),
        in_specs=[hbm] * len(args),
        out_specs=(pl.BlockSpec(memory_space=vmem),) * 2,
        scratch_shapes=scratch,
        compiler_params=pltpu.CompilerParams(
            collective_id=0, has_side_effects=True, vmem_limit_bytes=56 * 1024 * 1024
        ),
    )(*args)
    return pl.pallas_call(
        hand_over,
        out_shape=(
            jax.ShapeDtypeStruct((N, D), BF),
            jax.ShapeDtypeStruct((VN, D), BF),
        ),
        in_specs=[pl.BlockSpec(memory_space=vmem)] * 2,
        out_specs=(hbm, hbm),
        scratch_shapes=[dma((5,))],
        compiler_params=pltpu.CompilerParams(vmem_limit_bytes=16 * 1024 * 1024),
    )(node, virtual)


def solution(mesh):
    rows = P(("group", "dom"), None)
    line = P(("group", "dom"))
    placed = (
        rows, P(), P(), P(), P(), P(), P(), P(), P(), P(),
        rows, line, P(("group", "dom"), None, None), rows, line,
    )
    return jax.shard_map(
        shards, mesh=mesh, in_specs=placed, out_specs=(rows, P()), check_vma=False
    )
```
